32 devices in a mesh: bins: 4 (over y, core), batch: 8 (over z, x).
Axes of the slice: x: 2, y: 2, z: 4, core: 2. Of those that a mesh axis runs over, the one named last changes fastest.
Arguments:
- features: bfloat16 [8, 1024, 1536], P('batch', 'bins'), may hold values from -6 to 6
- norm_gain: float32 [1536], replicated, may hold values from 0.25 to 1.75
- convolution_taps_weight: bfloat16 [3, 1536, 768], replicated, may hold values from -0.09375 to 0.09375
- out_weight: bfloat16 [768, 1536], replicated, may hold values from -0.21875 to 0.21875
- head_weight: bfloat16 [1536, 4096], P(None, 'batch'), may hold values from -0.15625 to 0.15625
- rc_perm: int32 [1536], replicated, may hold values from 0 to 1535, each once
- exon_bins: int32 [8, 16, 8], P('batch'), may hold values from 0 to 1023, as said below
- exon_count: int32 [8, 16], P('batch'), may hold values from 1 to 8
- gene_strand: int32 [8, 16], P('batch'), may hold values 0 or 1
- gene_target: float32 [8, 16, 4096], P('batch', 'bins'), may hold values from 0.5 to 8
Outputs:
- input_grad: bfloat16 [8, 1024, 1536], P('batch', 'bins')
- out_weight_grad: float32 [768, 1536], P('batch')
The draws below stay inside these ranges and needn't reach their ends.
Inputs may be any that keep to these rules, and one draw needn't show every extreme that they name: `rc_perm`: a permutation of the channels. `exon_bins`: bins of the gene's own sequence; a bin may be listed more than once; each gene's listed bins lie within 256 consecutive bins. All genes of a sequence may lie within the same 256 bins j * 256 to (j + 1) * 256 - 1 of one j, and then every one of those bins may be listed and counted.
All inputs are finite; a program needn't handle non-finite values. No bound on the sum of `gene_strand` on one device may be relied on, other than what follows from the above.
Results may differ from the reference program's by a relative error of at most 0.014.
Values may be sent and summed in bfloat16 or wider, within the bound.
A program may use at most 128 MiB of HBM per device.

```python
import math
import jax
import jax.numpy as jnp
from jax import lax

C = 1536
H = 768
TR = 4096
DILATION_STEP = 16
EX = 8
LB = 256
L = 1024
G = 16
SEQS = 8


def exon_layout(key):
    folded = jax.random.fold_in(key, 911)
    key_list = jax.random.split(folded, 6)
    starts = jax.random.randint(key_list[0], (SEQS, G, 1), 0, L - LB + 1)
    offsets = jax.random.randint(key_list[1], (SEQS, G, EX), 0, LB)
    spread = starts + offsets
    chosen_sequence = jax.random.randint(key_list[2], (), 0, SEQS)
    chosen_block = jax.random.randint(key_list[3], (), 0, L // LB)
    rotation = jax.random.randint(key_list[4], (), 0, LB)
    listed = jnp.arange(G * EX, dtype=jnp.int32).reshape(G, EX)
    packed = (listed + rotation) % LB + chosen_block * LB
    clustered = jnp.arange(SEQS, dtype=jnp.int32) == chosen_sequence
    exon_list = jnp.where(clustered[:, None, None], packed[None, :, :], spread).astype(jnp.int32)
    counted = jax.random.randint(key_list[5], (SEQS, G), 1, EX + 1)
    counted = jnp.where(clustered[:, None], EX, counted).astype(jnp.int32)
    return (exon_list, counted)


def draw_exon_bins(key, part):
    return exon_layout(key)[0]


def draw_exon_count(key, part):
    return exon_layout(key)[1]


def with_ends(drawn, stream_key, low, top_value):
    longest = drawn.shape.index(max(drawn.shape))
    spots = []
    for shift in (0, 1):
        where = [jax.random.randint(jax.random.fold_in(stream_key, axis), (), 0, length) for axis, length in enumerate(drawn.shape)]
        where[longest] = (where[longest] + shift) % drawn.shape[longest]
        spots.append(tuple(where))
    return drawn.at[spots[0]].set(low).at[spots[1]].set(top_value)


def level_of(rng, shape, cuts, least, high):
    def one(position, blocks):
        heights = jax.random.uniform(jax.random.fold_in(jax.random.fold_in(rng, 6), position), (blocks,), jnp.float32, least / len(cuts), high / len(cuts))
        return jnp.repeat(jnp.exp(heights), shape[position] // blocks).reshape((-1,) + (1,) * (len(shape) - position - 1))

    level = one(*cuts[0])
    for cut in cuts[1:]:
        level = level * one(*cut)
    return level


def scatter_about(key, dims, scale, limit, cuts=(), kind=jnp.bfloat16):
    factor_of = level_of(key, dims, cuts, -0.22, 0.18) if cuts else 1.0
    drawn = jax.random.normal(key, dims, jnp.float32) * scale * factor_of
    return jnp.minimum(jnp.maximum(drawn, -limit), limit).astype(kind)


def setup_inputs(seed: int = 0) -> dict:
    streams_of = jax.random.split(jax.random.key(seed), 11)
    features = scatter_about(streams_of[0], (SEQS, L, C), 1.0, 6.0, ((0, 8), (1, 4)))
    norm_gain = jnp.clip(1.0 + 0.15 * jax.random.normal(streams_of[1], (C,), jnp.float32), 0.25, 1.75)
    convolution_taps_weight = scatter_about(streams_of[2], (3, C, H), (3 * C) ** -0.5, 0.09375)
    out_weight = scatter_about(streams_of[3], (H, C), H ** -0.5, 0.21875)
    head_weight = scatter_about(streams_of[4], (C, TR), C ** -0.5, 0.15625, ((1, 8),))
    rc_perm = jax.random.permutation(streams_of[5], C).astype(jnp.int32)
    exon_bins = draw_exon_bins(jax.random.fold_in(streams_of[10], 71), 0)
    exon_count = draw_exon_count(jax.random.fold_in(streams_of[10], 71), 0)
    gene_strand = with_ends((jax.random.randint(streams_of[8], (SEQS, G), 0, 2) < 1).astype(jnp.int32), jax.random.fold_in(streams_of[8], 1), 0, 1)
    gene_target = jnp.clip(jnp.exp(math.log(8.0) - 2.7725887 * jax.random.uniform(streams_of[9], (SEQS, G, TR), jnp.float32) ** level_of(streams_of[9], (SEQS, G, TR), ((0, 8), (1, 4)), -0.2, 0.2)), 0.5, 8.0)
    return dict(features=features, norm_gain=norm_gain, convolution_taps_weight=convolution_taps_weight, out_weight=out_weight, head_weight=head_weight, rc_perm=rc_perm, exon_bins=exon_bins, exon_count=exon_count, gene_strand=gene_strand, gene_target=gene_target)


def gelu_slope(argument):
    return 0.5 * (1.0 + jax.scipy.special.erf(argument * 0.7071067811865476)) + argument * jnp.exp(-0.5 * argument * argument) * 0.3989422804014327

def pair_flip(matrix, strand):
    swapped = matrix.reshape(matrix.shape[0], -1, 2)[:, :, ::-1].reshape(matrix.shape)
    return jnp.where(strand[:, None] == 1, swapped, matrix)

def exon_hits(bin_lists, counts, positions):
    listed = jnp.arange(bin_lists.shape[1], dtype=jnp.int32)[None, :] < counts[:, None]
    matched = (bin_lists[:, :, None] == positions[None, None, :]) & listed[:, :, None]
    return lax.optimization_barrier(jnp.sum(matched.astype(jnp.float32), axis=1)).astype(jnp.bfloat16)

def one_sequence(inputs, norm_gain, convolution_taps_weight, out_weight, head_weight, rc_perm, inverse_perm):
    features, bin_lists, counts, strand, target = inputs
    widened = features.astype(jnp.float32)
    count_of_rows = widened.shape[0]
    inverse = lax.rsqrt(lax.optimization_barrier(jnp.mean(widened * widened, axis=-1, keepdims=True)) + 1e-06)
    normed = widened * inverse * norm_gain
    hidden_state = jax.nn.gelu(normed, approximate=False).astype(jnp.bfloat16)
    padded_input = jnp.pad(hidden_state, ((DILATION_STEP, DILATION_STEP), (0, 0)))
    convolved_sum = jnp.zeros((count_of_rows, convolution_taps_weight.shape[2]), jnp.float32)
    for kernel_tap_index in range(3):
        convolved_sum = convolved_sum + jnp.dot(padded_input[kernel_tap_index * DILATION_STEP:kernel_tap_index * DILATION_STEP + count_of_rows], convolution_taps_weight[kernel_tap_index], preferred_element_type=jnp.float32)
    active = jax.nn.gelu(convolved_sum, approximate=False).astype(jnp.bfloat16)
    block_out = (widened + jnp.dot(active, out_weight, preferred_element_type=jnp.float32)).astype(jnp.bfloat16)
    logits = jnp.dot(block_out, head_weight, preferred_element_type=jnp.float32)
    predicted = jax.nn.softplus(logits).astype(jnp.bfloat16)
    positions = jnp.arange(count_of_rows, dtype=jnp.int32)
    hit_counts = exon_hits(bin_lists, counts, positions)
    partial_value = jnp.dot(hit_counts, predicted, preferred_element_type=jnp.float32)
    coverage = pair_flip(partial_value, strand)
    adjoint = (1.0 - target / (1.0 + coverage)).astype(jnp.bfloat16)
    spread_back = pair_flip(adjoint, strand)
    pred_grad = lax.dot_general(hit_counts, spread_back, (((0,), (0,)), ((), ())), preferred_element_type=jnp.float32)
    logit_grad = (pred_grad * jax.nn.sigmoid(logits)).astype(jnp.bfloat16)
    head_back = lax.dot_general(logit_grad, head_weight, (((1,), (1,)), ((), ())), preferred_element_type=jnp.float32)
    mirrored = block_out[::-1].astype(jnp.float32)
    block_wide = block_out.astype(jnp.float32)
    rc_grad = block_wide - 0.5 * (mirrored[:, rc_perm] + mirrored[:, inverse_perm])
    block_grad = (head_back + rc_grad).astype(jnp.bfloat16)
    weight_grad = lax.dot_general(active, block_grad, (((0,), (0,)), ((), ())), preferred_element_type=jnp.float32)
    activation_gradient = (lax.dot_general(block_grad, out_weight, (((1,), (1,)), ((), ())), preferred_element_type=jnp.float32) * gelu_slope(convolved_sum)).astype(jnp.bfloat16)
    padded_gradient = jnp.pad(activation_gradient, ((DILATION_STEP, DILATION_STEP), (0, 0)))
    hidden_grad = jnp.zeros((count_of_rows, convolution_taps_weight.shape[1]), jnp.float32)
    for kernel_tap_index in range(3):
        shift_amount = (2 - kernel_tap_index) * DILATION_STEP
        hidden_grad = hidden_grad + lax.dot_general(padded_gradient[shift_amount:shift_amount + count_of_rows], convolution_taps_weight[kernel_tap_index], (((1,), (1,)), ((), ())), preferred_element_type=jnp.float32)
    normed_grad = hidden_grad * gelu_slope(normed) * norm_gain
    norm_back = inverse * normed_grad - widened * inverse ** 3 * lax.optimization_barrier(jnp.mean(normed_grad * widened, axis=-1, keepdims=True))
    input_grad = (block_grad.astype(jnp.float32) + norm_back).astype(jnp.bfloat16)
    return (input_grad, weight_grad)

def reference(features, norm_gain, convolution_taps_weight, out_weight, head_weight, rc_perm, exon_bins, exon_count, gene_strand, gene_target):
    channels = rc_perm.shape[0]
    inverse_perm = jnp.zeros((channels,), jnp.int32).at[rc_perm].set(jnp.arange(channels, dtype=jnp.int32))

    def per_sequence(grad_total, inputs):
        input_grad, weight_grad = one_sequence(inputs, norm_gain, convolution_taps_weight, out_weight, head_weight, rc_perm, inverse_perm)
        return (grad_total + weight_grad, input_grad)
    start_total = jnp.zeros((out_weight.shape[0], out_weight.shape[1]), jnp.float32)
    grad_total, input_grads = lax.scan(per_sequence, start_total, (features, exon_bins, exon_count, gene_strand, gene_target))
    return (input_grads, grad_total)
```

```python
import functools

import jax
import jax.numpy as jnp
from jax import lax
from jax.experimental import pallas as pl
from jax.experimental.pallas import tpu as pltpu
from jax.sharding import PartitionSpec as P

DILATION_STEP = 16
MESH = pl.DeviceIdType.MESH
BF = jnp.bfloat16
F32 = jnp.float32


def greet(axis, count):
    me = lax.axis_index(axis)
    barrier = pltpu.get_barrier_semaphore()
    for step in range(1, count):
        pl.semaphore_signal(
            barrier,
            inc=1,
            device_id={axis: lax.rem(me + step, count)},
            device_id_type=MESH,
        )
    pl.semaphore_wait(barrier, count - 1)
    return me


def exchange_kernel(axis, count, x_ref, o_ref, local, send_sem, recv_sem):
    me = greet(axis, count)
    copies = []
    for step in range(1, count):
        peer = lax.rem(me + step, count)
        copy = pltpu.make_async_remote_copy(
            src_ref=x_ref.at[peer],
            dst_ref=o_ref.at[me],
            send_sem=send_sem.at[step],
            recv_sem=recv_sem.at[step],
            device_id={axis: peer},
            device_id_type=MESH,
        )
        copy.start()
        copies.append(copy)
    mine = pltpu.make_async_copy(x_ref.at[me], o_ref.at[me], local)
    mine.start()
    mine.wait()
    for copy in copies:
        copy.wait()


def gather_kernel(axis, count, x_ref, o_ref, local, send_sem, recv_sem):
    me = greet(axis, count)
    copies = []
    for step in range(1, count):
        peer = lax.rem(me + step, count)
        copy = pltpu.make_async_remote_copy(
            src_ref=x_ref,
            dst_ref=o_ref.at[me],
            send_sem=send_sem.at[step],
            recv_sem=recv_sem.at[step],
            device_id={axis: peer},
            device_id_type=MESH,
        )
        copy.start()
        copies.append(copy)
    mine = pltpu.make_async_copy(x_ref, o_ref.at[me], local)
    mine.start()
    mine.wait()
    for copy in copies:
        copy.wait()


def reduce_kernel(axis, count, x_ref, o_ref, held, send_sem, recv_sem):
    me = greet(axis, count)
    copies = []
    for step in range(1, count):
        peer = lax.rem(me + step, count)
        copy = pltpu.make_async_remote_copy(
            src_ref=x_ref.at[peer],
            dst_ref=held.at[step],
            send_sem=send_sem.at[step],
            recv_sem=recv_sem.at[step],
            device_id={axis: peer},
            device_id_type=MESH,
        )
        copy.start()
        copies.append(copy)
    total = x_ref[me].astype(F32)
    for step in range(1, count):
        copies[step - 1].wait_recv()
        total = total + held[step].astype(F32)
    o_ref[...] = total.astype(o_ref.dtype)
    for copy in copies:
        copy.wait_send()


def vmem():
    return pl.BlockSpec(memory_space=pltpu.VMEM)


def run(kernel, x, out, scratch, collective_id, count):
    return pl.pallas_call(
        kernel,
        out_shape=out,
        in_specs=[vmem()],
        out_specs=vmem(),
        scratch_shapes=[
            scratch,
            pltpu.SemaphoreType.DMA((count,)),
            pltpu.SemaphoreType.DMA((count,)),
        ],
        compiler_params=pltpu.CompilerParams(
            collective_id=collective_id,
            has_side_effects=True,
            vmem_limit_bytes=32 * 1024 * 1024,
        ),
    )(x)


def exchange(x, axis, cid):
    count = lax.axis_size(axis)
    return run(
        functools.partial(exchange_kernel, axis, count),
        x,
        jax.ShapeDtypeStruct(x.shape, x.dtype),
        pltpu.SemaphoreType.DMA,
        cid,
        count,
    )


def gather(x, axis, cid):
    count = lax.axis_size(axis)
    return run(
        functools.partial(gather_kernel, axis, count),
        x,
        jax.ShapeDtypeStruct((count,) + x.shape, x.dtype),
        pltpu.SemaphoreType.DMA,
        cid,
        count,
    )


def reduce_pieces(x, axis, cid):
    count = lax.axis_size(axis)
    return run(
        functools.partial(reduce_kernel, axis, count),
        x,
        jax.ShapeDtypeStruct(x.shape[1:], x.dtype),
        pltpu.VMEM(x.shape, x.dtype),
        cid,
        count,
    )


def with_halo(block, axis, width):
    count = lax.axis_size(axis)
    forward = [(i, i + 1) for i in range(count - 1)]
    backward = [(target, source) for source, target in forward]
    low = lax.ppermute(block[-width:], axis, forward)
    high = lax.ppermute(block[:width], axis, backward)
    return jnp.concatenate([low, block, high], axis=0)


def gelu_slope(argument):
    return (
        0.5 * (1.0 + jax.scipy.special.erf(argument * 0.7071067811865476))
        + argument * jnp.exp(-0.5 * argument * argument) * 0.3989422804014327
    )


def dot(a, b, dims=((1,), (0,))):
    return lax.dot_general(a, b, (dims, ((), ())), preferred_element_type=F32)


def per_device(
    features,
    norm_gain,
    taps,
    out_weight,
    head_weight,
    rc_perm,
    exon_bins,
    exon_count,
    gene_strand,
    gene_target,
):
    bin_devices = lax.axis_size("bins")
    batch_devices = lax.axis_size("batch")
    bin_index = lax.axis_index("bins")
    rows, channels = features.shape[1:]
    hid = taps.shape[2]
    genes, exons = exon_bins.shape[1:]
    own_genes = gene_target.shape[1]
    tracks = gene_target.shape[2]
    part = head_weight.shape[1]
    own_rows = own_genes * exons

    own_strand = lax.dynamic_slice_in_dim(gene_strand[0], bin_index * own_genes, own_genes, 0)
    own_count = lax.dynamic_slice_in_dim(exon_count[0], bin_index * own_genes, own_genes, 0)
    target = gene_target[0]
    lane = lax.broadcasted_iota(jnp.int32, target.shape, 1)
    swapped = jnp.where(lane % 2 == 0, jnp.roll(target, -1, axis=1), jnp.roll(target, 1, axis=1))
    target = jnp.where(own_strand[:, None] == 1, swapped, target)
    pieces = target.reshape(own_genes, batch_devices, part).transpose(1, 0, 2)
    counted = jnp.broadcast_to(
        own_count.astype(F32)[None, :, None], (batch_devices, own_genes, 128)
    )
    arrived = exchange(jnp.concatenate([pieces, counted], axis=2), "batch", 1)
    track_target = arrived[:, :, :part]
    track_count = arrived[:, :, part : part + 1].astype(jnp.int32)

    widened = features[0].astype(F32)
    inverse = lax.rsqrt(jnp.mean(widened * widened, axis=-1, keepdims=True) + 1e-06)
    normed = widened * inverse * norm_gain
    hidden = jax.nn.gelu(normed, approximate=False).astype(BF)
    padded = with_halo(hidden, "bins", DILATION_STEP)
    conv_sum = jnp.zeros((rows, hid), F32)
    for tap in range(3):
        conv_sum = conv_sum + dot(
            padded[tap * DILATION_STEP : tap * DILATION_STEP + rows], taps[tap]
        )
    active = jax.nn.gelu(conv_sum, approximate=False).astype(BF)
    block_out = (widened + dot(active, out_weight)).astype(BF)

    partner = lax.ppermute(
        block_out, "bins", [(i, bin_devices - 1 - i) for i in range(bin_devices)]
    )

    positions = bin_index * rows + jnp.arange(rows, dtype=jnp.int32)
    listed = jnp.arange(exons, dtype=jnp.int32)[None, :] < exon_count[0][:, None]
    hits = (
        (exon_bins[0][:, :, None] == positions[None, None, :]) & listed[:, :, None]
    ).reshape(genes * exons, rows).astype(BF)
    picked = dot(hits, block_out).astype(BF).reshape(bin_devices, own_rows, channels)
    own_picked = reduce_pieces(picked, "bins", 2)
    all_picked = gather(own_picked, "batch", 3).reshape(batch_devices * own_rows, channels)

    logits = dot(all_picked, head_weight).reshape(batch_devices, own_genes, exons, part)
    predicted = jax.nn.softplus(logits).astype(BF).astype(F32)
    counts = lax.broadcasted_iota(jnp.int32, (1, 1, exons, 1), 2) < track_count[..., None]
    partial = jnp.sum(jnp.where(counts, predicted, 0.0), axis=2)
    spread = (1.0 - track_target / (1.0 + partial)).astype(BF).astype(F32)
    logit_grad = jnp.where(counts, spread[:, :, None, :] * jax.nn.sigmoid(logits), 0.0).astype(BF)
    picked_grad = dot(
        logit_grad.reshape(batch_devices * own_rows, part), head_weight, ((1,), (1,))
    ).astype(BF).reshape(batch_devices, own_rows, channels)
    own_grad = reduce_pieces(picked_grad, "batch", 4)
    seq_grad = gather(own_grad, "bins", 5).reshape(genes * exons, channels)
    head_back = dot(hits, seq_grad, ((0,), (0,)))

    flip = (
        lax.broadcasted_iota(jnp.int32, (rows, rows), 0)
        == rows - 1 - lax.broadcasted_iota(jnp.int32, (rows, rows), 1)
    ).astype(BF)
    down = lax.broadcasted_iota(jnp.int32, (channels, channels), 0)
    along = lax.broadcasted_iota(jnp.int32, (channels, channels), 1)
    both_maps = (
        (down == rc_perm[None, :]).astype(F32) + (rc_perm[:, None] == along).astype(F32)
    ).astype(BF)
    mirrored = dot(flip, partner).astype(BF)
    rc_grad = block_out.astype(F32) - 0.5 * dot(mirrored, both_maps)
    block_grad = (head_back + rc_grad).astype(BF)

    act_grad = (dot(block_grad, out_weight, ((1,), (1,))) * gelu_slope(conv_sum)).astype(BF)
    padded_grad = with_halo(act_grad, "bins", DILATION_STEP)

    weight_terms = dot(active, block_grad, ((0,), (0,))).astype(BF)
    wide = channels // bin_devices
    weight_terms = weight_terms.reshape(hid, bin_devices, wide).transpose(1, 0, 2)
    bins_sum = reduce_pieces(weight_terms, "bins", 6)
    own_sum = reduce_pieces(
        bins_sum.reshape(batch_devices, hid // batch_devices, wide), "batch", 7
    )
    out_weight_grad = gather(own_sum, "bins", 8).transpose(1, 0, 2)
    out_weight_grad = out_weight_grad.reshape(hid // batch_devices, channels).astype(F32)

    hidden_grad = jnp.zeros((rows, channels), F32)
    for tap in range(3):
        shift = (2 - tap) * DILATION_STEP
        hidden_grad = hidden_grad + dot(
            padded_grad[shift : shift + rows], taps[tap], ((1,), (1,))
        )
    normed_grad = hidden_grad * gelu_slope(normed) * norm_gain
    norm_back = inverse * normed_grad - widened * inverse**3 * jnp.mean(
        normed_grad * widened, axis=-1, keepdims=True
    )
    input_grad = (block_grad.astype(F32) + norm_back).astype(BF)
    return (input_grad[None], out_weight_grad)


def solution(mesh):
    in_specs = (
        P("batch", "bins", None),
        P(),
        P(),
        P(),
        P(None, "batch"),
        P(),
        P("batch", None, None),
        P("batch", None),
        P("batch", None),
        P("batch", "bins", None),
    )
    out_specs = (P("batch", "bins", None), P("batch", None))
    return jax.shard_map(
        per_device, mesh=mesh, in_specs=in_specs, out_specs=out_specs, check_vma=False
    )
```

```python
import functools

import jax
import jax.numpy as jnp
from jax import lax
from jax.experimental import pallas as pl
from jax.experimental.pallas import tpu as pltpu
from jax.sharding import PartitionSpec as P

DILATION_STEP = 16
MESH = pl.DeviceIdType.MESH
BF = jnp.bfloat16
F32 = jnp.float32


def place(axis, stride):
    index = lax.axis_index(axis)
    me = lax.div(index, stride)
    rest = lax.rem(index, stride)
    return me, lambda at: at * stride + rest


def greet(axis, devices):
    barrier = pltpu.get_barrier_semaphore()
    for device in devices:
        pl.semaphore_signal(barrier, inc=1, device_id={axis: device}, device_id_type=MESH)
    pl.semaphore_wait(barrier, len(devices))


def join(axis, stride, count):
    me, at = place(axis, stride)
    greet(axis, [at(lax.rem(me + step, count)) for step in range(1, count)])
    return me, at


def exchange_kernel(axis, stride, count, x_ref, o_ref, local, send_sem, recv_sem):
    me, at = join(axis, stride, count)
    copies = []
    for step in range(1, count):
        peer = lax.rem(me + step, count)
        copy = pltpu.make_async_remote_copy(
            src_ref=x_ref.at[peer],
            dst_ref=o_ref.at[me],
            send_sem=send_sem.at[step],
            recv_sem=recv_sem.at[step],
            device_id={axis: at(peer)},
            device_id_type=MESH,
        )
        copy.start()
        copies.append(copy)
    mine = pltpu.make_async_copy(x_ref.at[me], o_ref.at[me], local)
    mine.start()
    mine.wait()
    for copy in copies:
        copy.wait()


def gather_kernel(axis, stride, count, x_ref, o_ref, local, send_sem, recv_sem):
    me, at = join(axis, stride, count)
    copies = []
    for step in range(1, count):
        peer = lax.rem(me + step, count)
        copy = pltpu.make_async_remote_copy(
            src_ref=x_ref,
            dst_ref=o_ref.at[me],
            send_sem=send_sem.at[step],
            recv_sem=recv_sem.at[step],
            device_id={axis: at(peer)},
            device_id_type=MESH,
        )
        copy.start()
        copies.append(copy)
    mine = pltpu.make_async_copy(x_ref, o_ref.at[me], local)
    mine.start()
    mine.wait()
    for copy in copies:
        copy.wait()


def reduce_kernel(axis, stride, count, x_ref, o_ref, held, send_sem, recv_sem):
    me, at = join(axis, stride, count)
    copies = []
    for step in range(1, count):
        peer = lax.rem(me + step, count)
        copy = pltpu.make_async_remote_copy(
            src_ref=x_ref.at[peer],
            dst_ref=held.at[step],
            send_sem=send_sem.at[step],
            recv_sem=recv_sem.at[step],
            device_id={axis: at(peer)},
            device_id_type=MESH,
        )
        copy.start()
        copies.append(copy)
    total = x_ref[me].astype(F32)
    for step in range(1, count):
        copies[step - 1].wait_recv()
        total = total + held[step].astype(F32)
    o_ref[...] = total.astype(o_ref.dtype)
    for copy in copies:
        copy.wait_send()


def vmem():
    return pl.BlockSpec(memory_space=pltpu.VMEM)


def run(kernel, x, out, scratch, collective_id, count):
    return pl.pallas_call(
        kernel,
        out_shape=out,
        in_specs=[vmem()],
        out_specs=vmem(),
        scratch_shapes=[
            scratch,
            pltpu.SemaphoreType.DMA((count,)),
            pltpu.SemaphoreType.DMA((count,)),
        ],
        compiler_params=pltpu.CompilerParams(
            collective_id=collective_id,
            has_side_effects=True,
            vmem_limit_bytes=32 * 1024 * 1024,
        ),
    )(x)


def exchange(x, axis, cid, stride=1):
    count = lax.axis_size(axis) // stride
    return run(
        functools.partial(exchange_kernel, axis, stride, count),
        x,
        jax.ShapeDtypeStruct(x.shape, x.dtype),
        pltpu.SemaphoreType.DMA,
        cid,
        count,
    )


def gather(x, axis, cid, stride=1):
    count = lax.axis_size(axis) // stride
    return run(
        functools.partial(gather_kernel, axis, stride, count),
        x,
        jax.ShapeDtypeStruct((count,) + x.shape, x.dtype),
        pltpu.SemaphoreType.DMA,
        cid,
        count,
    )


def reduce_pieces(x, axis, cid, stride=1):
    count = lax.axis_size(axis) // stride
    return run(
        functools.partial(reduce_kernel, axis, stride, count),
        x,
        jax.ShapeDtypeStruct(x.shape[1:], x.dtype),
        pltpu.VMEM(x.shape, x.dtype),
        cid,
        count,
    )


def weight_kernel(
    axis, count, a_ref, g_ref, o_ref, out1, in1, out2, in2, send1, recv1, send2, recv2
):
    me = lax.axis_index(axis)
    half = count // 2
    spot, parity = lax.div(me, 2), lax.rem(me, 2)
    buddy = 2 * spot + 1 - parity
    quarters = [lax.rem(spot + step, half) for step in range(half)]
    greet(axis, [buddy] + [2 * quarters[step] + parity for step in range(1, half)])

    def term(part):
        return lax.dot_general(
            a_ref[...], g_ref[part], (((0,), (0,)), ((), ())), preferred_element_type=F32
        )

    order = list(range(1, half)) + [0]
    first = {}
    for step in order:
        out1[step] = term(2 * quarters[step] + 1 - parity).astype(BF)
        first[step] = pltpu.make_async_remote_copy(
            src_ref=out1.at[step],
            dst_ref=in1.at[step],
            send_sem=send1.at[step],
            recv_sem=recv1.at[step],
            device_id={axis: buddy},
            device_id_type=MESH,
        )
        first[step].start()
    second = {}
    for step in order:
        total = term(2 * quarters[step] + parity)
        first[step].wait_recv()
        total = total + in1[step].astype(F32)
        if step:
            out2[step] = total.astype(BF)
            second[step] = pltpu.make_async_remote_copy(
                src_ref=out2.at[step],
                dst_ref=in2.at[step],
                send_sem=send2.at[step],
                recv_sem=recv2.at[step],
                device_id={axis: 2 * quarters[step] + parity},
                device_id_type=MESH,
            )
            second[step].start()
    for step in range(1, half):
        second[step].wait_recv()
        total = total + in2[step].astype(F32)
    o_ref[...] = total.astype(o_ref.dtype)
    for step in range(half):
        first[step].wait_send()
    for step in range(1, half):
        second[step].wait_send()


def weight_sum(active, grad, axis, cid):
    count, rows, wide = grad.shape
    hid = active.shape[1]
    half = count // 2
    return pl.pallas_call(
        functools.partial(weight_kernel, axis, count),
        out_shape=jax.ShapeDtypeStruct((hid, wide), BF),
        in_specs=[vmem(), vmem()],
        out_specs=vmem(),
        scratch_shapes=[pltpu.VMEM((half, hid, wide), BF) for _ in range(4)]
        + [pltpu.SemaphoreType.DMA((half,)) for _ in range(4)],
        compiler_params=pltpu.CompilerParams(
            collective_id=cid, has_side_effects=True, vmem_limit_bytes=32 * 1024 * 1024
        ),
    )(active, grad)


def with_halo(block, axis, width):
    count = lax.axis_size(axis)
    forward = [(i, i + 1) for i in range(count - 1)]
    backward = [(target, source) for source, target in forward]
    low = lax.ppermute(block[-width:], axis, forward)
    high = lax.ppermute(block[:width], axis, backward)
    return jnp.concatenate([low, block, high], axis=0)


def gelu_slope(argument):
    return (
        0.5 * (1.0 + jax.scipy.special.erf(argument * 0.7071067811865476))
        + argument * jnp.exp(-0.5 * argument * argument) * 0.3989422804014327
    )


def dot(a, b, dims=((1,), (0,))):
    return lax.dot_general(a, b, (dims, ((), ())), preferred_element_type=F32)


def per_device(
    features,
    norm_gain,
    taps,
    out_weight,
    head_weight,
    rc_perm,
    exon_bins,
    exon_count,
    gene_strand,
    gene_target,
):
    bin_devices = lax.axis_size("bins")
    batch_devices = lax.axis_size("batch")
    bin_index = lax.axis_index("bins")
    rows, channels = features.shape[1:]
    hid = taps.shape[2]
    genes, exons = exon_bins.shape[1:]
    own_genes = gene_target.shape[1]
    tracks = gene_target.shape[2]
    part = head_weight.shape[1]
    own_rows = own_genes * exons

    other_head = lax.ppermute(
        head_weight, "batch", [(i, i ^ 1) for i in range(batch_devices)]
    )
    own_strand = lax.dynamic_slice_in_dim(gene_strand[0], bin_index * own_genes, own_genes, 0)
    own_count = lax.dynamic_slice_in_dim(exon_count[0], bin_index * own_genes, own_genes, 0)
    target = gene_target[0]
    lane = lax.broadcasted_iota(jnp.int32, target.shape, 1)
    swapped = jnp.where(lane % 2 == 0, jnp.roll(target, -1, axis=1), jnp.roll(target, 1, axis=1))
    target = jnp.where(own_strand[:, None] == 1, swapped, target)
    pairs = batch_devices // 2
    odd = lax.rem(lax.axis_index("batch"), 2)
    pieces = target.reshape(own_genes, pairs, 2, part)
    pieces = jnp.where(odd == 1, pieces[:, :, ::-1], pieces)
    pieces = pieces.reshape(own_genes, pairs, 2 * part).transpose(1, 0, 2)
    counted = jnp.broadcast_to(own_count.astype(F32)[None, :, None], (pairs, own_genes, 128))
    arrived = exchange(jnp.concatenate([pieces, counted], axis=2), "batch", 1, 2)
    track_target = arrived[:, :, : 2 * part]
    track_count = arrived[:, :, 2 * part : 2 * part + 1].astype(jnp.int32)

    widened = features[0].astype(F32)
    inverse = lax.rsqrt(jnp.mean(widened * widened, axis=-1, keepdims=True) + 1e-06)
    normed = widened * inverse * norm_gain
    hidden = jax.nn.gelu(normed, approximate=False).astype(BF)
    padded = with_halo(hidden, "bins", DILATION_STEP)
    conv_sum = jnp.zeros((rows, hid), F32)
    for tap in range(3):
        conv_sum = conv_sum + dot(
            padded[tap * DILATION_STEP : tap * DILATION_STEP + rows], taps[tap]
        )
    active = jax.nn.gelu(conv_sum, approximate=False).astype(BF)
    block_out = (widened + dot(active, out_weight)).astype(BF)

    positions = bin_index * rows + jnp.arange(rows, dtype=jnp.int32)
    listed = jnp.arange(exons, dtype=jnp.int32)[None, :] < exon_count[0][:, None]
    hits = (
        (exon_bins[0][:, :, None] == positions[None, None, :]) & listed[:, :, None]
    ).reshape(genes * exons, rows).astype(BF)
    picked = dot(hits, block_out).astype(BF).reshape(bin_devices, own_rows, channels)
    own_picked = reduce_pieces(picked, "bins", 2)
    own_picked, block_out = lax.optimization_barrier((own_picked, block_out))
    partner = lax.ppermute(
        block_out, "bins", [(i, bin_devices - 1 - i) for i in range(bin_devices)]
    )
    all_picked = gather(own_picked, "batch", 3, 2).reshape(pairs * own_rows, channels)

    logits = jnp.concatenate([dot(all_picked, head_weight), dot(all_picked, other_head)], axis=1)
    logits = logits.reshape(pairs, own_genes, exons, 2 * part)
    predicted = jax.nn.softplus(logits).astype(BF).astype(F32)
    counts = lax.broadcasted_iota(jnp.int32, (1, 1, exons, 1), 2) < track_count[..., None]
    partial = jnp.sum(jnp.where(counts, predicted, 0.0), axis=2)
    spread = (1.0 - track_target / (1.0 + partial)).astype(BF).astype(F32)
    logit_grad = jnp.where(counts, spread[:, :, None, :] * jax.nn.sigmoid(logits), 0.0).astype(BF)
    logit_grad = logit_grad.reshape(pairs * own_rows, 2 * part)
    picked_grad = dot(logit_grad[:, :part], head_weight, ((1,), (1,))) + dot(
        logit_grad[:, part:], other_head, ((1,), (1,))
    )
    picked_grad = picked_grad.astype(BF).reshape(pairs, own_rows, channels)
    own_grad = reduce_pieces(picked_grad, "batch", 4, 2)
    seq_grad = gather(own_grad, "bins", 5).reshape(genes * exons, channels)
    head_back = dot(hits, seq_grad, ((0,), (0,)))

    flip = (
        lax.broadcasted_iota(jnp.int32, (rows, rows), 0)
        == rows - 1 - lax.broadcasted_iota(jnp.int32, (rows, rows), 1)
    ).astype(BF)
    down = lax.broadcasted_iota(jnp.int32, (channels, channels), 0)
    along = lax.broadcasted_iota(jnp.int32, (channels, channels), 1)
    both_maps = (
        (down == rc_perm[None, :]).astype(F32) + (rc_perm[:, None] == along).astype(F32)
    ).astype(BF)
    mirrored = dot(flip, partner).astype(BF)
    rc_grad = block_out.astype(F32) - 0.5 * dot(mirrored, both_maps)
    block_grad = (head_back + rc_grad).astype(BF)

    act_grad = (dot(block_grad, out_weight, ((1,), (1,))) * gelu_slope(conv_sum)).astype(BF)
    padded_grad = with_halo(act_grad, "bins", DILATION_STEP)

    wide = channels // bin_devices
    bins_sum = weight_sum(
        active, block_grad.reshape(rows, bin_devices, wide).transpose(1, 0, 2), "bins", 6
    )
    own_sum = reduce_pieces(
        bins_sum.reshape(batch_devices, hid // batch_devices, wide), "batch", 7
    )
    out_weight_grad = gather(own_sum, "bins", 8).transpose(1, 0, 2)
    out_weight_grad = out_weight_grad.reshape(hid // batch_devices, channels).astype(F32)

    hidden_grad = jnp.zeros((rows, channels), F32)
    for tap in range(3):
        shift = (2 - tap) * DILATION_STEP
        hidden_grad = hidden_grad + dot(
            padded_grad[shift : shift + rows], taps[tap], ((1,), (1,))
        )
    normed_grad = hidden_grad * gelu_slope(normed) * norm_gain
    norm_back = inverse * normed_grad - widened * inverse**3 * jnp.mean(
        normed_grad * widened, axis=-1, keepdims=True
    )
    input_grad = (block_grad.astype(F32) + norm_back).astype(BF)
    return (input_grad[None], out_weight_grad)


def solution(mesh):
    in_specs = (
        P("batch", "bins", None),
        P(),
        P(),
        P(),
        P(None, "batch"),
        P(),
        P("batch", None, None),
        P("batch", None),
        P("batch", None),
        P("batch", "bins", None),
    )
    out_specs = (P("batch", "bins", None), P("batch", None))
    return jax.shard_map(
        per_device, mesh=mesh, in_specs=in_specs, out_specs=out_specs, check_vma=False
    )
```

```python
import functools

import jax
import jax.numpy as jnp
from jax import lax
from jax.experimental import pallas as pl
from jax.experimental.pallas import tpu as pltpu
from jax.sharding import PartitionSpec as P

DILATION_STEP = 16
MESH = pl.DeviceIdType.MESH
BF = jnp.bfloat16
F32 = jnp.float32


def place(axis, stride):
    index = lax.axis_index(axis)
    me = lax.div(index, stride)
    rest = lax.rem(index, stride)
    return me, lambda at: at * stride + rest


def greet(axis, devices):
    barrier = pltpu.get_barrier_semaphore()
    for device in devices:
        pl.semaphore_signal(barrier, inc=1, device_id={axis: device}, device_id_type=MESH)
    pl.semaphore_wait(barrier, len(devices))


def join(axis, stride, count):
    me, at = place(axis, stride)
    greet(axis, [at(lax.rem(me + step, count)) for step in range(1, count)])
    return me, at


def gather_kernel(axis, stride, count, x_ref, o_ref, local, send_sem, recv_sem):
    me, at = join(axis, stride, count)
    copies = []
    for step in range(1, count):
        peer = lax.rem(me + step, count)
        copy = pltpu.make_async_remote_copy(
            src_ref=x_ref,
            dst_ref=o_ref.at[me],
            send_sem=send_sem.at[step],
            recv_sem=recv_sem.at[step],
            device_id={axis: at(peer)},
            device_id_type=MESH,
        )
        copy.start()
        copies.append(copy)
    mine = pltpu.make_async_copy(x_ref, o_ref.at[me], local)
    mine.start()
    mine.wait()
    for copy in copies:
        copy.wait()


def reduce_kernel(axis, stride, count, x_ref, o_ref, held, send_sem, recv_sem):
    me, at = join(axis, stride, count)
    copies = []
    for step in range(1, count):
        peer = lax.rem(me + step, count)
        copy = pltpu.make_async_remote_copy(
            src_ref=x_ref.at[peer],
            dst_ref=held.at[step],
            send_sem=send_sem.at[step],
            recv_sem=recv_sem.at[step],
            device_id={axis: at(peer)},
            device_id_type=MESH,
        )
        copy.start()
        copies.append(copy)
    total = x_ref[me].astype(F32)
    for step in range(1, count):
        copies[step - 1].wait_recv()
        total = total + held[step].astype(F32)
    o_ref[...] = total.astype(o_ref.dtype)
    for copy in copies:
        copy.wait_send()


def vmem():
    return pl.BlockSpec(memory_space=pltpu.VMEM)


def run(kernel, x, out, scratch, collective_id, count):
    return pl.pallas_call(
        kernel,
        out_shape=out,
        in_specs=[vmem()],
        out_specs=vmem(),
        scratch_shapes=[
            scratch,
            pltpu.SemaphoreType.DMA((count,)),
            pltpu.SemaphoreType.DMA((count,)),
        ],
        compiler_params=pltpu.CompilerParams(
            collective_id=collective_id,
            has_side_effects=True,
            vmem_limit_bytes=32 * 1024 * 1024,
        ),
    )(x)


def gather(x, axis, cid, stride=1):
    count = lax.axis_size(axis) // stride
    return run(
        functools.partial(gather_kernel, axis, stride, count),
        x,
        jax.ShapeDtypeStruct((count,) + x.shape, x.dtype),
        pltpu.SemaphoreType.DMA,
        cid,
        count,
    )


def reduce_pieces(x, axis, cid, stride=1):
    count = lax.axis_size(axis) // stride
    return run(
        functools.partial(reduce_kernel, axis, stride, count),
        x,
        jax.ShapeDtypeStruct(x.shape[1:], x.dtype),
        pltpu.VMEM(x.shape, x.dtype),
        cid,
        count,
    )


def gelu_slope(argument):
    return (
        0.5 * (1.0 + jax.scipy.special.erf(argument * 0.7071067811865476))
        + argument * jnp.exp(-0.5 * argument * argument) * 0.3989422804014327
    )


def dot(a, b, dims=((1,), (0,))):
    return lax.dot_general(a, b, (dims, ((), ())), preferred_element_type=F32)


ROOT_HALF = 0.7071067811865476


def gelu(v):
    return 0.5 * v * (1.0 + lax.erf(v * ROOT_HALF))


def send(src, dst, send_sem, recv_sem, device):
    copy = pltpu.make_async_remote_copy(
        src_ref=src,
        dst_ref=dst,
        send_sem=send_sem,
        recv_sem=recv_sem,
        device_id=device,
        device_id_type=MESH,
    )
    copy.start()
    return copy


def halo_copies(pad, rows, count, sems):
    me = lax.axis_index("bins")
    step = DILATION_STEP
    up = pltpu.make_async_remote_copy(
        src_ref=pad.at[pl.ds(rows, step)],
        dst_ref=pad.at[pl.ds(0, step)],
        send_sem=sems.at[0],
        recv_sem=sems.at[1],
        device_id={"bins": lax.rem(me + 1, count)},
        device_id_type=MESH,
    )
    down = pltpu.make_async_remote_copy(
        src_ref=pad.at[pl.ds(step, step)],
        dst_ref=pad.at[pl.ds(rows + step, step)],
        send_sem=sems.at[2],
        recv_sem=sems.at[3],
        device_id={"bins": lax.rem(me + count - 1, count)},
        device_id_type=MESH,
    )
    return up, down


def halo_start(pad, rows, count, sems):
    me = lax.axis_index("bins")
    up, down = halo_copies(pad, rows, count, sems)

    @pl.when(me < count - 1)
    def _():
        up.start()

    @pl.when(me > 0)
    def _():
        down.start()

    @pl.when(me == 0)
    def _():
        pad[0:DILATION_STEP] = jnp.zeros((DILATION_STEP, pad.shape[1]), pad.dtype)

    @pl.when(me == count - 1)
    def _():
        pad[rows + DILATION_STEP : rows + 2 * DILATION_STEP] = jnp.zeros(
            (DILATION_STEP, pad.shape[1]), pad.dtype
        )


def halo_wait(pad, rows, count, sems):
    me = lax.axis_index("bins")
    up, down = halo_copies(pad, rows, count, sems)

    @pl.when(me < count - 1)
    def _():
        up.wait_send()
        down.wait_recv()

    @pl.when(me > 0)
    def _():
        down.wait_send()
        up.wait_recv()


def meet(groups):
    barrier = pltpu.get_barrier_semaphore()
    total = 0
    for axis, devices in groups:
        total += len(devices)
        for device in devices:
            pl.semaphore_signal(barrier, inc=1, device_id={axis: device}, device_id_type=MESH)
    pl.semaphore_wait(barrier, total)


def front_kernel(
    count, pairs, f_ref, gain_ref, taps_ref, ow_ref, hits_ref, goal_ref,
    conv_ref, active_ref, out_ref, all_ref, arrived_ref,
    pad, picked, held, own, halo_sem, local, send_a, recv_a, send_b, recv_b, send_c, recv_c,
):
    rows, channels = f_ref.shape
    hid = ow_ref.shape[0]
    own_rows = own.shape[0]
    step = DILATION_STEP
    me = lax.axis_index("bins")
    spot, at = place("batch", 2)
    others = [lax.rem(me + s, count) for s in range(1, count)]
    peers = [lax.rem(spot + s, pairs) for s in range(1, pairs)]
    meet([("bins", others), ("batch", [at(p) for p in peers])])

    goals = [
        send(goal_ref.at[p], arrived_ref.at[spot], send_a.at[i], recv_a.at[i], {"batch": at(p)})
        for i, p in enumerate(peers)
    ]
    mine = pltpu.make_async_copy(goal_ref.at[spot], arrived_ref.at[spot], local)
    mine.start()

    def norm(i):
        here = pl.ds(pl.multiple_of(i * step, step), step)
        wide = f_ref[here, :].astype(F32)
        inverse = lax.rsqrt(jnp.mean(wide * wide, axis=-1, keepdims=True) + 1e-06)
        pad[pl.ds(pl.multiple_of(i * step + step, step), step), :] = gelu(
            wide * inverse * gain_ref[...]
        ).astype(BF)

    norm(0)
    norm(rows // step - 1)
    halo_start(pad, rows, count, halo_sem)
    pl.loop(1, rows // step - 1)(norm)
    halo_wait(pad, rows, count, halo_sem)

    @pl.loop(0, hid // 256)
    def _(i):
        here = pl.ds(pl.multiple_of(i * 256, 256), 256)
        total = jnp.zeros((rows, 256), F32)
        for tap in range(3):
            total = total + dot(pad[tap * step : tap * step + rows, :], taps_ref[tap, :, here])
        conv_ref[:, here] = total
        active_ref[:, here] = gelu(total).astype(BF)

    @pl.loop(0, channels // 256)
    def _(i):
        here = pl.ds(pl.multiple_of(i * 256, 256), 256)
        block = f_ref[:, here].astype(F32) + dot(active_ref[...], ow_ref[:, here])
        block = block.astype(BF)
        out_ref[:, here] = block
        rows_of = dot(hits_ref[...], block).astype(BF)
        for j in range(count):
            picked[j, :, here] = rows_of[j * own_rows : (j + 1) * own_rows]

    legs = [
        send(picked.at[p], held.at[i], send_b.at[i], recv_b.at[i], {"bins": p})
        for i, p in enumerate(others)
    ]
    total = picked[me].astype(F32)
    for i, leg in enumerate(legs):
        leg.wait_recv()
        total = total + held[i].astype(F32)
    own[...] = total.astype(BF)
    spread = [
        send(own, all_ref.at[spot], send_c.at[i], recv_c.at[i], {"batch": at(p)})
        for i, p in enumerate(peers)
    ]
    all_ref[spot] = own[...]
    mine.wait()
    for leg in legs:
        leg.wait_send()
    for copy in goals + spread:
        copy.wait()


def front(features, gain, taps, out_weight, hits, goals):
    count = lax.axis_size("bins")
    pairs = goals.shape[0]
    rows, channels = features.shape
    hid = out_weight.shape[0]
    own_rows = hits.shape[0] // count
    dma = pltpu.SemaphoreType.DMA
    return pl.pallas_call(
        functools.partial(front_kernel, count, pairs),
        out_shape=(
            jax.ShapeDtypeStruct((rows, hid), F32),
            jax.ShapeDtypeStruct((rows, hid), BF),
            jax.ShapeDtypeStruct((rows, channels), BF),
            jax.ShapeDtypeStruct((pairs, own_rows, channels), BF),
            jax.ShapeDtypeStruct(goals.shape, F32),
        ),
        in_specs=[vmem()] * 6,
        out_specs=(vmem(),) * 5,
        scratch_shapes=[
            pltpu.VMEM((rows + 2 * DILATION_STEP, channels), BF),
            pltpu.VMEM((count, own_rows, channels), BF),
            pltpu.VMEM((count, own_rows, channels), BF),
            pltpu.VMEM((own_rows, channels), BF),
            dma((4,)),
            dma,
            dma((pairs,)),
            dma((pairs,)),
            dma((count,)),
            dma((count,)),
            dma((pairs,)),
            dma((pairs,)),
        ],
        compiler_params=pltpu.CompilerParams(
            collective_id=1, has_side_effects=True, vmem_limit_bytes=48 * 1024 * 1024
        ),
    )(features, gain.reshape(1, channels), taps, out_weight, hits, goals)


def tail_kernel(
    count, batch, f_ref, gain_ref, taps_ref, ow_ref, conv_ref, a_ref, g_ref, parts_ref,
    ig_ref, og_ref,
    pad, hidden_grad, out1, in1, out2, in2, bsum, held, osum,
    halo_sem, send1, recv1, send2, recv2, send3, recv3, send4, recv4,
):
    rows, channels = f_ref.shape
    hid = ow_ref.shape[0]
    high = osum.shape[0]
    step_rows = DILATION_STEP
    me = lax.axis_index("bins")
    seq = lax.axis_index("batch")
    others = [lax.rem(me + s, count) for s in range(1, count)]
    peers = [lax.rem(seq + s, batch) for s in range(1, batch)]
    meet([("bins", others), ("batch", peers)])
    half = count // 2
    spot, parity = lax.div(me, 2), lax.rem(me, 2)
    buddy = 2 * spot + 1 - parity
    quarters = [lax.rem(spot + step, half) for step in range(half)]
    order = list(range(1, half)) + [0]

    def term(part):
        return dot(a_ref[...], parts_ref[part], ((0,), (0,)))

    first = {}
    for step in order:
        out1[step] = term(2 * quarters[step] + 1 - parity).astype(BF)
        first[step] = send(
            out1.at[step], in1.at[step], send1.at[step], recv1.at[step], {"bins": buddy}
        )

    @pl.loop(0, hid // 256)
    def _(i):
        here = pl.ds(pl.multiple_of(i * 256, 256), 256)
        grad = dot(g_ref[...], ow_ref[here, :], ((1,), (1,))) * gelu_slope(conv_ref[:, here])
        pad[step_rows : step_rows + rows, here] = grad.astype(BF)

    halo_start(pad, rows, count, halo_sem)

    second = {}
    for step in order:
        total = term(2 * quarters[step] + parity)
        first[step].wait_recv()
        total = total + in1[step].astype(F32)
        if step:
            out2[step] = total.astype(BF)
            second[step] = send(
                out2.at[step],
                in2.at[step],
                send2.at[step],
                recv2.at[step],
                {"bins": 2 * quarters[step] + parity},
            )
        else:
            out2[0] = total.astype(BF)

    halo_wait(pad, rows, count, halo_sem)

    @pl.loop(0, channels // 256)
    def _(i):
        here = pl.ds(pl.multiple_of(i * 256, 256), 256)
        total = jnp.zeros((rows, 256), F32)
        for tap in range(3):
            shift = (2 - tap) * step_rows
            total = total + dot(
                pad[shift : shift + rows, :], taps_ref[tap, here, :], ((1,), (1,))
            )
        hidden_grad[:, here] = total

    @pl.loop(0, rows // step_rows)
    def _(i):
        here = pl.ds(pl.multiple_of(i * step_rows, step_rows), step_rows)
        wide = f_ref[here, :].astype(F32)
        inverse = lax.rsqrt(jnp.mean(wide * wide, axis=-1, keepdims=True) + 1e-06)
        gain = gain_ref[...]
        normed_grad = hidden_grad[here, :] * gelu_slope(wide * inverse * gain) * gain
        back = inverse * normed_grad - wide * (inverse * inverse * inverse) * jnp.mean(
            normed_grad * wide, axis=-1, keepdims=True
        )
        ig_ref[here, :] = (g_ref[here, :].astype(F32) + back).astype(BF)

    for step in range(1, half):
        second[step].wait_recv()
    for j in range(batch):
        part = out2[0, j * high : (j + 1) * high].astype(F32)
        for step in range(1, half):
            part = part + in2[step, j * high : (j + 1) * high].astype(F32)
        bsum[j] = part.astype(BF)
    third = [
        send(bsum.at[p], held.at[i], send3.at[i], recv3.at[i], {"batch": p})
        for i, p in enumerate(peers)
    ]
    total = bsum[seq].astype(F32)
    for i, copy in enumerate(third):
        copy.wait_recv()
        total = total + held[i].astype(F32)
    osum[...] = total.astype(BF)
    fourth = [
        send(osum, og_ref.at[me], send4.at[i], recv4.at[i], {"bins": p})
        for i, p in enumerate(others)
    ]
    og_ref[me] = osum[...]
    for step in range(half):
        first[step].wait_send()
    for step in range(1, half):
        second[step].wait_send()
    for copy in third:
        copy.wait_send()
    for copy in fourth:
        copy.wait()


def tail(features, gain, taps, out_weight, conv_sum, active, grad, parts):
    count, rows, wide = parts.shape
    batch = lax.axis_size("batch")
    channels = features.shape[1]
    hid = active.shape[1]
    half = count // 2
    high = hid // batch
    dma = pltpu.SemaphoreType.DMA
    return pl.pallas_call(
        functools.partial(tail_kernel, count, batch),
        out_shape=(
            jax.ShapeDtypeStruct((rows, channels), BF),
            jax.ShapeDtypeStruct((count, high, wide), BF),
        ),
        in_specs=[vmem()] * 8,
        out_specs=(vmem(),) * 2,
        scratch_shapes=[
            pltpu.VMEM((rows + 2 * DILATION_STEP, hid), BF),
            pltpu.VMEM((rows, channels), F32),
        ]
        + [pltpu.VMEM((half, hid, wide), BF) for _ in range(4)]
        + [
            pltpu.VMEM((batch, high, wide), BF),
            pltpu.VMEM((batch, high, wide), BF),
            pltpu.VMEM((high, wide), BF),
            dma((4,)),
        ]
        + [dma((half,)) for _ in range(4)]
        + [dma((batch,)) for _ in range(2)]
        + [dma((count,)) for _ in range(2)],
        compiler_params=pltpu.CompilerParams(
            collective_id=6, has_side_effects=True, vmem_limit_bytes=56 * 1024 * 1024
        ),
    )(features, gain.reshape(1, channels), taps, out_weight, conv_sum, active, grad, parts)


def per_device(
    features,
    norm_gain,
    taps,
    out_weight,
    head_weight,
    rc_perm,
    exon_bins,
    exon_count,
    gene_strand,
    gene_target,
):
    bin_devices = lax.axis_size("bins")
    batch_devices = lax.axis_size("batch")
    bin_index = lax.axis_index("bins")
    rows, channels = features.shape[1:]
    hid = taps.shape[2]
    genes, exons = exon_bins.shape[1:]
    own_genes = gene_target.shape[1]
    tracks = gene_target.shape[2]
    part = head_weight.shape[1]
    own_rows = own_genes * exons

    other_head = lax.ppermute(
        head_weight, "batch", [(i, i ^ 1) for i in range(batch_devices)]
    )
    own_strand = lax.dynamic_slice_in_dim(gene_strand[0], bin_index * own_genes, own_genes, 0)
    own_count = lax.dynamic_slice_in_dim(exon_count[0], bin_index * own_genes, own_genes, 0)
    target = gene_target[0]
    lane = lax.broadcasted_iota(jnp.int32, target.shape, 1)
    swapped = jnp.where(lane % 2 == 0, jnp.roll(target, -1, axis=1), jnp.roll(target, 1, axis=1))
    target = jnp.where(own_strand[:, None] == 1, swapped, target)
    pairs = batch_devices // 2
    odd = lax.rem(lax.axis_index("batch"), 2)
    pieces = target.reshape(own_genes, pairs, 2, part)
    pieces = jnp.where(odd == 1, pieces[:, :, ::-1], pieces)
    pieces = pieces.reshape(own_genes, pairs, 2 * part).transpose(1, 0, 2)
    counted = jnp.broadcast_to(own_count.astype(F32)[None, :, None], (pairs, own_genes, 128))
    positions = bin_index * rows + jnp.arange(rows, dtype=jnp.int32)
    listed = jnp.arange(exons, dtype=jnp.int32)[None, :] < exon_count[0][:, None]
    hits = (
        (exon_bins[0][:, :, None] == positions[None, None, :]) & listed[:, :, None]
    ).reshape(genes * exons, rows).astype(BF)
    conv_sum, active, block_out, all_picked, arrived = front(
        features[0], norm_gain, taps, out_weight, hits, jnp.concatenate([pieces, counted], axis=2)
    )
    track_target = arrived[:, :, : 2 * part]
    track_count = arrived[:, :, 2 * part : 2 * part + 1].astype(jnp.int32)
    partner = lax.ppermute(
        block_out, "bins", [(i, bin_devices - 1 - i) for i in range(bin_devices)]
    )
    all_picked = all_picked.reshape(pairs * own_rows, channels)

    logits = jnp.concatenate([dot(all_picked, head_weight), dot(all_picked, other_head)], axis=1)
    logits = logits.reshape(pairs, own_genes, exons, 2 * part)
    predicted = jax.nn.softplus(logits).astype(BF).astype(F32)
    counts = lax.broadcasted_iota(jnp.int32, (1, 1, exons, 1), 2) < track_count[..., None]
    partial = jnp.sum(jnp.where(counts, predicted, 0.0), axis=2)
    spread = (1.0 - track_target / (1.0 + partial)).astype(BF).astype(F32)
    logit_grad = jnp.where(counts, spread[:, :, None, :] * jax.nn.sigmoid(logits), 0.0).astype(BF)
    logit_grad = logit_grad.reshape(pairs * own_rows, 2 * part)
    picked_grad = dot(logit_grad[:, :part], head_weight, ((1,), (1,))) + dot(
        logit_grad[:, part:], other_head, ((1,), (1,))
    )
    picked_grad = picked_grad.astype(BF).reshape(pairs, own_rows, channels)
    own_grad = reduce_pieces(picked_grad, "batch", 4, 2)
    seq_grad = gather(own_grad, "bins", 5).reshape(genes * exons, channels)
    head_back = dot(hits, seq_grad, ((0,), (0,)))

    flip = (
        lax.broadcasted_iota(jnp.int32, (rows, rows), 0)
        == rows - 1 - lax.broadcasted_iota(jnp.int32, (rows, rows), 1)
    ).astype(BF)
    down = lax.broadcasted_iota(jnp.int32, (channels, channels), 0)
    along = lax.broadcasted_iota(jnp.int32, (channels, channels), 1)
    both_maps = (
        (down == rc_perm[None, :]).astype(F32) + (rc_perm[:, None] == along).astype(F32)
    ).astype(BF)
    mirrored = dot(flip, partner).astype(BF)
    rc_grad = block_out.astype(F32) - 0.5 * dot(mirrored, both_maps)
    block_grad = (head_back + rc_grad).astype(BF)

    wide = channels // bin_devices
    input_grad, own_parts = tail(
        features[0],
        norm_gain,
        taps,
        out_weight,
        conv_sum,
        active,
        block_grad,
        block_grad.reshape(rows, bin_devices, wide).transpose(1, 0, 2),
    )
    out_weight_grad = own_parts.transpose(1, 0, 2).reshape(hid // batch_devices, channels)
    out_weight_grad = out_weight_grad.astype(F32)
    return (input_grad[None], out_weight_grad)


def solution(mesh):
    in_specs = (
        P("batch", "bins", None),
        P(),
        P(),
        P(),
        P(None, "batch"),
        P(),
        P("batch", None, None),
        P("batch", None),
        P("batch", None),
        P("batch", "bins", None),
    )
    out_specs = (P("batch", "bins", None), P("batch", None))
    return jax.shard_map(
        per_device, mesh=mesh, in_specs=in_specs, out_specs=out_specs, check_vma=False
    )
```

```python
import functools

import jax
import jax.numpy as jnp
from jax import lax
from jax.experimental import pallas as pl
from jax.experimental.pallas import tpu as pltpu
from jax.sharding import PartitionSpec as P

DILATION_STEP = 16
MESH = pl.DeviceIdType.MESH
BF = jnp.bfloat16
F32 = jnp.float32


def place(axis, stride):
    index = lax.axis_index(axis)
    me = lax.div(index, stride)
    rest = lax.rem(index, stride)
    return me, lambda at: at * stride + rest


def vmem():
    return pl.BlockSpec(memory_space=pltpu.VMEM)


def gelu_slope(argument):
    return (
        0.5 * (1.0 + jax.scipy.special.erf(argument * 0.7071067811865476))
        + argument * jnp.exp(-0.5 * argument * argument) * 0.3989422804014327
    )


def dot(a, b, dims=((1,), (0,))):
    return lax.dot_general(a, b, (dims, ((), ())), preferred_element_type=F32)


ROOT_HALF = 0.7071067811865476


def gelu(v):
    return 0.5 * v * (1.0 + lax.erf(v * ROOT_HALF))


def send(src, dst, send_sem, recv_sem, device):
    copy = pltpu.make_async_remote_copy(
        src_ref=src,
        dst_ref=dst,
        send_sem=send_sem,
        recv_sem=recv_sem,
        device_id=device,
        device_id_type=MESH,
    )
    copy.start()
    return copy


def halo_copies(pad, rows, count, sems):
    me = lax.axis_index("bins")
    step = DILATION_STEP
    up = pltpu.make_async_remote_copy(
        src_ref=pad.at[pl.ds(rows, step)],
        dst_ref=pad.at[pl.ds(0, step)],
        send_sem=sems.at[0],
        recv_sem=sems.at[1],
        device_id={"bins": lax.rem(me + 1, count)},
        device_id_type=MESH,
    )
    down = pltpu.make_async_remote_copy(
        src_ref=pad.at[pl.ds(step, step)],
        dst_ref=pad.at[pl.ds(rows + step, step)],
        send_sem=sems.at[2],
        recv_sem=sems.at[3],
        device_id={"bins": lax.rem(me + count - 1, count)},
        device_id_type=MESH,
    )
    return up, down


def halo_start(pad, rows, count, sems):
    me = lax.axis_index("bins")
    up, down = halo_copies(pad, rows, count, sems)

    @pl.when(me < count - 1)
    def _():
        up.start()

    @pl.when(me > 0)
    def _():
        down.start()

    @pl.when(me == 0)
    def _():
        pad[0:DILATION_STEP] = jnp.zeros((DILATION_STEP, pad.shape[1]), pad.dtype)

    @pl.when(me == count - 1)
    def _():
        pad[rows + DILATION_STEP : rows + 2 * DILATION_STEP] = jnp.zeros(
            (DILATION_STEP, pad.shape[1]), pad.dtype
        )


def halo_wait(pad, rows, count, sems):
    me = lax.axis_index("bins")
    up, down = halo_copies(pad, rows, count, sems)

    @pl.when(me < count - 1)
    def _():
        up.wait_send()
        down.wait_recv()

    @pl.when(me > 0)
    def _():
        down.wait_send()
        up.wait_recv()


def meet(groups):
    barrier = pltpu.get_barrier_semaphore()
    total = 0
    for axis, devices in groups:
        total += len(devices)
        for device in devices:
            pl.semaphore_signal(barrier, inc=1, device_id={axis: device}, device_id_type=MESH)
    pl.semaphore_wait(barrier, total)


def front_kernel(
    count, pairs, f_ref, gain_ref, taps_ref, ow_ref, hits_ref, goal_ref,
    conv_ref, active_ref, out_ref, all_ref, arrived_ref,
    pad, picked, held, own, halo_sem, local, send_a, recv_a, send_b, recv_b, send_c, recv_c,
):
    rows, channels = f_ref.shape
    hid = ow_ref.shape[0]
    own_rows = own.shape[0]
    step = DILATION_STEP
    me = lax.axis_index("bins")
    spot, at = place("batch", 2)
    others = [lax.rem(me + s, count) for s in range(1, count)]
    peers = [lax.rem(spot + s, pairs) for s in range(1, pairs)]
    meet([("bins", others), ("batch", [at(p) for p in peers])])

    goals = [
        send(goal_ref.at[p], arrived_ref.at[spot], send_a.at[i], recv_a.at[i], {"batch": at(p)})
        for i, p in enumerate(peers)
    ]
    mine = pltpu.make_async_copy(goal_ref.at[spot], arrived_ref.at[spot], local)
    mine.start()

    def norm(i):
        here = pl.ds(pl.multiple_of(i * step, step), step)
        wide = f_ref[here, :].astype(F32)
        inverse = lax.rsqrt(jnp.mean(wide * wide, axis=-1, keepdims=True) + 1e-06)
        pad[pl.ds(pl.multiple_of(i * step + step, step), step), :] = gelu(
            wide * inverse * gain_ref[...]
        ).astype(BF)

    norm(0)
    norm(rows // step - 1)
    halo_start(pad, rows, count, halo_sem)
    pl.loop(1, rows // step - 1)(norm)
    halo_wait(pad, rows, count, halo_sem)

    @pl.loop(0, hid // 256)
    def _(i):
        here = pl.ds(pl.multiple_of(i * 256, 256), 256)
        total = jnp.zeros((rows, 256), F32)
        for tap in range(3):
            total = total + dot(pad[tap * step : tap * step + rows, :], taps_ref[tap, :, here])
        conv_ref[:, here] = total
        active_ref[:, here] = gelu(total).astype(BF)

    @pl.loop(0, channels // 256)
    def _(i):
        here = pl.ds(pl.multiple_of(i * 256, 256), 256)
        block = f_ref[:, here].astype(F32) + dot(active_ref[...], ow_ref[:, here])
        block = block.astype(BF)
        out_ref[:, here] = block
        rows_of = dot(hits_ref[...], block).astype(BF)
        for j in range(count):
            picked[j, :, here] = rows_of[j * own_rows : (j + 1) * own_rows]

    legs = [
        send(picked.at[p], held.at[i], send_b.at[i], recv_b.at[i], {"bins": p})
        for i, p in enumerate(others)
    ]
    total = picked[me].astype(F32)
    for i, leg in enumerate(legs):
        leg.wait_recv()
        total = total + held[i].astype(F32)
    own[...] = total.astype(BF)
    spread = [
        send(own, all_ref.at[spot], send_c.at[i], recv_c.at[i], {"batch": at(p)})
        for i, p in enumerate(peers)
    ]
    all_ref[spot] = own[...]
    mine.wait()
    for leg in legs:
        leg.wait_send()
    for copy in goals + spread:
        copy.wait()


def front(features, gain, taps, out_weight, hits, goals):
    count = lax.axis_size("bins")
    pairs = goals.shape[0]
    rows, channels = features.shape
    hid = out_weight.shape[0]
    own_rows = hits.shape[0] // count
    dma = pltpu.SemaphoreType.DMA
    return pl.pallas_call(
        functools.partial(front_kernel, count, pairs),
        out_shape=(
            jax.ShapeDtypeStruct((rows, hid), F32),
            jax.ShapeDtypeStruct((rows, hid), BF),
            jax.ShapeDtypeStruct((rows, channels), BF),
            jax.ShapeDtypeStruct((pairs, own_rows, channels), BF),
            jax.ShapeDtypeStruct(goals.shape, F32),
        ),
        in_specs=[vmem()] * 6,
        out_specs=(vmem(),) * 5,
        scratch_shapes=[
            pltpu.VMEM((rows + 2 * DILATION_STEP, channels), BF),
            pltpu.VMEM((count, own_rows, channels), BF),
            pltpu.VMEM((count, own_rows, channels), BF),
            pltpu.VMEM((own_rows, channels), BF),
            dma((4,)),
            dma,
            dma((pairs,)),
            dma((pairs,)),
            dma((count,)),
            dma((count,)),
            dma((pairs,)),
            dma((pairs,)),
        ],
        compiler_params=pltpu.CompilerParams(
            collective_id=1, has_side_effects=True, vmem_limit_bytes=48 * 1024 * 1024
        ),
    )(features, gain.reshape(1, channels), taps, out_weight, hits, goals)


def tail_kernel(
    count, batch, f_ref, gain_ref, taps_ref, ow_ref, conv_ref, a_ref, g_ref, parts_ref,
    ig_ref, og_ref,
    pad, hidden_grad, out1, in1, out2, in2, bsum, held, osum,
    halo_sem, send1, recv1, send2, recv2, send3, recv3, send4, recv4,
):
    rows, channels = f_ref.shape
    hid = ow_ref.shape[0]
    high = osum.shape[0]
    step_rows = DILATION_STEP
    me = lax.axis_index("bins")
    seq = lax.axis_index("batch")
    others = [lax.rem(me + s, count) for s in range(1, count)]
    peers = [lax.rem(seq + s, batch) for s in range(1, batch)]
    meet([("bins", others), ("batch", peers)])
    half = count // 2
    spot, parity = lax.div(me, 2), lax.rem(me, 2)
    buddy = 2 * spot + 1 - parity
    quarters = [lax.rem(spot + step, half) for step in range(half)]
    order = list(range(1, half)) + [0]

    def term(part):
        return dot(a_ref[...], parts_ref[part], ((0,), (0,)))

    first = {}
    for step in order:
        out1[step] = term(2 * quarters[step] + 1 - parity).astype(BF)
        first[step] = send(
            out1.at[step], in1.at[step], send1.at[step], recv1.at[step], {"bins": buddy}
        )

    @pl.loop(0, hid // 256)
    def _(i):
        here = pl.ds(pl.multiple_of(i * 256, 256), 256)
        grad = dot(g_ref[...], ow_ref[here, :], ((1,), (1,))) * gelu_slope(conv_ref[:, here])
        pad[step_rows : step_rows + rows, here] = grad.astype(BF)

    halo_start(pad, rows, count, halo_sem)

    second = {}
    for step in order:
        total = term(2 * quarters[step] + parity)
        first[step].wait_recv()
        total = total + in1[step].astype(F32)
        if step:
            out2[step] = total.astype(BF)
            second[step] = send(
                out2.at[step],
                in2.at[step],
                send2.at[step],
                recv2.at[step],
                {"bins": 2 * quarters[step] + parity},
            )
        else:
            out2[0] = total.astype(BF)

    halo_wait(pad, rows, count, halo_sem)

    @pl.loop(0, channels // 256)
    def _(i):
        here = pl.ds(pl.multiple_of(i * 256, 256), 256)
        total = jnp.zeros((rows, 256), F32)
        for tap in range(3):
            shift = (2 - tap) * step_rows
            total = total + dot(
                pad[shift : shift + rows, :], taps_ref[tap, here, :], ((1,), (1,))
            )
        hidden_grad[:, here] = total

    @pl.loop(0, rows // step_rows)
    def _(i):
        here = pl.ds(pl.multiple_of(i * step_rows, step_rows), step_rows)
        wide = f_ref[here, :].astype(F32)
        inverse = lax.rsqrt(jnp.mean(wide * wide, axis=-1, keepdims=True) + 1e-06)
        gain = gain_ref[...]
        normed_grad = hidden_grad[here, :] * gelu_slope(wide * inverse * gain) * gain
        back = inverse * normed_grad - wide * (inverse * inverse * inverse) * jnp.mean(
            normed_grad * wide, axis=-1, keepdims=True
        )
        ig_ref[here, :] = (g_ref[here, :].astype(F32) + back).astype(BF)

    for step in range(1, half):
        second[step].wait_recv()
    for j in range(batch):
        part = out2[0, j * high : (j + 1) * high].astype(F32)
        for step in range(1, half):
            part = part + in2[step, j * high : (j + 1) * high].astype(F32)
        bsum[j] = part.astype(BF)
    third = [
        send(bsum.at[p], held.at[i], send3.at[i], recv3.at[i], {"batch": p})
        for i, p in enumerate(peers)
    ]
    total = bsum[seq].astype(F32)
    for i, copy in enumerate(third):
        copy.wait_recv()
        total = total + held[i].astype(F32)
    osum[...] = total.astype(BF)
    fourth = [
        send(osum, og_ref.at[me], send4.at[i], recv4.at[i], {"bins": p})
        for i, p in enumerate(others)
    ]
    og_ref[me] = osum[...]
    for step in range(half):
        first[step].wait_send()
    for step in range(1, half):
        second[step].wait_send()
    for copy in third:
        copy.wait_send()
    for copy in fourth:
        copy.wait()


def tail(features, gain, taps, out_weight, conv_sum, active, grad, parts):
    count, rows, wide = parts.shape
    batch = lax.axis_size("batch")
    channels = features.shape[1]
    hid = active.shape[1]
    half = count // 2
    high = hid // batch
    dma = pltpu.SemaphoreType.DMA
    return pl.pallas_call(
        functools.partial(tail_kernel, count, batch),
        out_shape=(
            jax.ShapeDtypeStruct((rows, channels), BF),
            jax.ShapeDtypeStruct((count, high, wide), BF),
        ),
        in_specs=[vmem()] * 8,
        out_specs=(vmem(),) * 2,
        scratch_shapes=[
            pltpu.VMEM((rows + 2 * DILATION_STEP, hid), BF),
            pltpu.VMEM((rows, channels), F32),
        ]
        + [pltpu.VMEM((half, hid, wide), BF) for _ in range(4)]
        + [
            pltpu.VMEM((batch, high, wide), BF),
            pltpu.VMEM((batch, high, wide), BF),
            pltpu.VMEM((high, wide), BF),
            dma((4,)),
        ]
        + [dma((half,)) for _ in range(4)]
        + [dma((batch,)) for _ in range(2)]
        + [dma((count,)) for _ in range(2)],
        compiler_params=pltpu.CompilerParams(
            collective_id=6, has_side_effects=True, vmem_limit_bytes=56 * 1024 * 1024
        ),
    )(features, gain.reshape(1, channels), taps, out_weight, conv_sum, active, grad, parts)


def middle_kernel(
    count, pairs, out_ref, all_ref, head_ref, other_ref, goal_ref, sums_ref, hits_ref,
    perm_row_ref, perm_col_ref,
    bg_ref, parts_ref,
    partner, maps, rowgrad, pieces, held, own, seq, mirrored,
    send_m, recv_m, send_a, recv_a, send_b, recv_b,
):
    rows, channels = out_ref.shape
    part = head_ref.shape[1]
    own_rows = own.shape[0]
    wide = parts_ref.shape[2]
    me = lax.axis_index("bins")
    spot, at = place("batch", 2)
    others = [lax.rem(me + s, count) for s in range(1, count)]
    peers = [lax.rem(spot + s, pairs) for s in range(1, pairs)]
    meet([("bins", others), ("batch", [at(p) for p in peers])])

    mirror = send(out_ref, partner, send_m, recv_m, {"bins": count - 1 - me})

    picked = all_ref[...].reshape(pairs * own_rows, channels)
    for side, weight in enumerate((head_ref, other_ref)):
        logits = dot(picked, weight[...])
        predicted = jnp.maximum(logits, 0.0) + jnp.log1p(jnp.exp(-jnp.abs(logits)))
        covered = dot(sums_ref[...], predicted.astype(BF))
        goal = goal_ref[:, side * part : (side + 1) * part]
        spread = (1.0 - goal / (1.0 + covered)).astype(BF)
        back = dot(sums_ref[...], spread, ((0,), (0,)))
        rowgrad[side] = (back * jax.nn.sigmoid(logits)).astype(BF)

    @pl.loop(0, channels // 256)
    def _(i):
        here = pl.ds(pl.multiple_of(i * 256, 256), 256)
        grad = dot(rowgrad[0], head_ref[here, :], ((1,), (1,)))
        grad = (grad + dot(rowgrad[1], other_ref[here, :], ((1,), (1,)))).astype(BF)
        for j in range(pairs):
            pieces[j, :, here] = grad[j * own_rows : (j + 1) * own_rows]

    legs = [
        send(pieces.at[p], held.at[i], send_a.at[i], recv_a.at[i], {"batch": at(p)})
        for i, p in enumerate(peers)
    ]

    @pl.loop(0, channels // 256)
    def _(i):
        here = pl.ds(pl.multiple_of(i * 256, 256), 256)
        down = lax.broadcasted_iota(jnp.int32, (channels, 256), 0)
        along = lax.broadcasted_iota(jnp.int32, (channels, 256), 1) + i * 256
        first = jnp.where(down == perm_row_ref[:, here], 1.0, 0.0)
        second = jnp.where(along == perm_col_ref[...], 1.0, 0.0)
        maps[:, here] = (first + second).astype(BF)

    total = pieces[spot].astype(F32)
    for i, leg in enumerate(legs):
        leg.wait_recv()
        total = total + held[i].astype(F32)
    own[...] = total.astype(BF)
    spread_out = [
        send(own, seq.at[me], send_b.at[i], recv_b.at[i], {"bins": p})
        for i, p in enumerate(others)
    ]
    seq[me] = own[...]

    mirror.wait()
    flip = jnp.where(
        lax.broadcasted_iota(jnp.int32, (rows, rows), 0)
        + lax.broadcasted_iota(jnp.int32, (rows, rows), 1)
        == rows - 1,
        1.0,
        0.0,
    ).astype(BF)
    mirrored[...] = dot(flip, partner[...]).astype(BF)
    for copy in spread_out:
        copy.wait()

    @pl.loop(0, channels // 256)
    def _(i):
        here = pl.ds(pl.multiple_of(i * 256, 256), 256)
        grads = seq[:, :, here].reshape(count * own_rows, 256)
        block = dot(hits_ref[...], grads, ((0,), (0,))) + out_ref[:, here].astype(F32)
        bg_ref[:, here] = (block - 0.5 * dot(mirrored[...], maps[:, here])).astype(BF)

    for j in range(count):
        parts_ref[j] = bg_ref[:, j * wide : (j + 1) * wide]
    for leg in legs:
        leg.wait_send()


def middle(block_out, all_picked, head, other, goals, sums, hits, perm):
    count = lax.axis_size("bins")
    pairs, own_rows, channels = all_picked.shape
    rows = block_out.shape[0]
    part = head.shape[1]
    dma = pltpu.SemaphoreType.DMA
    return pl.pallas_call(
        functools.partial(middle_kernel, count, pairs),
        out_shape=(
            jax.ShapeDtypeStruct((rows, channels), BF),
            jax.ShapeDtypeStruct((count, rows, channels // count), BF),
        ),
        in_specs=[vmem()] * 9,
        out_specs=(vmem(),) * 2,
        scratch_shapes=[
            pltpu.VMEM((rows, channels), BF),
            pltpu.VMEM((channels, channels), BF),
            pltpu.VMEM((2, pairs * own_rows, part), BF),
            pltpu.VMEM((pairs, own_rows, channels), BF),
            pltpu.VMEM((pairs, own_rows, channels), BF),
            pltpu.VMEM((own_rows, channels), BF),
            pltpu.VMEM((count, own_rows, channels), BF),
            pltpu.VMEM((rows, channels), BF),
            dma,
            dma,
            dma((pairs,)),
            dma((pairs,)),
            dma((count,)),
            dma((count,)),
        ],
        compiler_params=pltpu.CompilerParams(
            collective_id=3, has_side_effects=True, vmem_limit_bytes=48 * 1024 * 1024
        ),
    )(
        block_out, all_picked, head, other, goals, sums, hits,
        perm.reshape(1, channels), perm.reshape(channels, 1),
    )


def per_device(
    features,
    norm_gain,
    taps,
    out_weight,
    head_weight,
    rc_perm,
    exon_bins,
    exon_count,
    gene_strand,
    gene_target,
):
    bin_devices = lax.axis_size("bins")
    batch_devices = lax.axis_size("batch")
    bin_index = lax.axis_index("bins")
    rows, channels = features.shape[1:]
    hid = taps.shape[2]
    genes, exons = exon_bins.shape[1:]
    own_genes = gene_target.shape[1]
    tracks = gene_target.shape[2]
    part = head_weight.shape[1]
    own_rows = own_genes * exons

    other_head = lax.ppermute(
        head_weight, "batch", [(i, i ^ 1) for i in range(batch_devices)]
    )
    own_strand = lax.dynamic_slice_in_dim(gene_strand[0], bin_index * own_genes, own_genes, 0)
    own_count = lax.dynamic_slice_in_dim(exon_count[0], bin_index * own_genes, own_genes, 0)
    target = gene_target[0]
    lane = lax.broadcasted_iota(jnp.int32, target.shape, 1)
    swapped = jnp.where(lane % 2 == 0, jnp.roll(target, -1, axis=1), jnp.roll(target, 1, axis=1))
    target = jnp.where(own_strand[:, None] == 1, swapped, target)
    pairs = batch_devices // 2
    odd = lax.rem(lax.axis_index("batch"), 2)
    pieces = target.reshape(own_genes, pairs, 2, part)
    pieces = jnp.where(odd == 1, pieces[:, :, ::-1], pieces)
    pieces = pieces.reshape(own_genes, pairs, 2 * part).transpose(1, 0, 2)
    counted = jnp.broadcast_to(own_count.astype(F32)[None, :, None], (pairs, own_genes, 128))
    positions = bin_index * rows + jnp.arange(rows, dtype=jnp.int32)
    listed = jnp.arange(exons, dtype=jnp.int32)[None, :] < exon_count[0][:, None]
    hits = (
        (exon_bins[0][:, :, None] == positions[None, None, :]) & listed[:, :, None]
    ).reshape(genes * exons, rows).astype(BF)
    conv_sum, active, block_out, all_picked, arrived = front(
        features[0], norm_gain, taps, out_weight, hits, jnp.concatenate([pieces, counted], axis=2)
    )
    gene_rows = pairs * own_genes
    goals = arrived[:, :, : 2 * part].reshape(gene_rows, 2 * part)
    row_count = arrived[:, :, 2 * part].reshape(gene_rows, 1).astype(jnp.int32)
    row = lax.broadcasted_iota(jnp.int32, (gene_rows, gene_rows * exons), 1)
    gene = lax.broadcasted_iota(jnp.int32, (gene_rows, gene_rows * exons), 0)
    sums = ((row // exons == gene) & (row % exons < row_count)).astype(BF)
    block_grad, grad_parts = middle(
        block_out, all_picked, head_weight, other_head, goals, sums, hits, rc_perm
    )
    input_grad, own_parts = tail(
        features[0],
        norm_gain,
        taps,
        out_weight,
        conv_sum,
        active,
        block_grad,
        grad_parts,
    )
    out_weight_grad = own_parts.transpose(1, 0, 2).reshape(hid // batch_devices, channels)
    out_weight_grad = out_weight_grad.astype(F32)
    return (input_grad[None], out_weight_grad)


def solution(mesh):
    in_specs = (
        P("batch", "bins", None),
        P(),
        P(),
        P(),
        P(None, "batch"),
        P(),
        P("batch", None, None),
        P("batch", None),
        P("batch", None),
        P("batch", "bins", None),
    )
    out_specs = (P("batch", "bins", None), P("batch", None))
    return jax.shard_map(
        per_device, mesh=mesh, in_specs=in_specs, out_specs=out_specs, check_vma=False
    )
```

```python
import functools

import jax
import jax.numpy as jnp
from jax import lax
from jax.experimental import pallas as pl
from jax.experimental.pallas import tpu as pltpu
from jax.sharding import PartitionSpec as P

DILATION_STEP = 16
MESH = pl.DeviceIdType.MESH
BF = jnp.bfloat16
F32 = jnp.float32


def place(axis, stride):
    index = lax.axis_index(axis)
    me = lax.div(index, stride)
    rest = lax.rem(index, stride)
    return me, lambda at: at * stride + rest


def vmem():
    return pl.BlockSpec(memory_space=pltpu.VMEM)


def gelu_slope(argument):
    return (
        0.5 * (1.0 + jax.scipy.special.erf(argument * 0.7071067811865476))
        + argument * jnp.exp(-0.5 * argument * argument) * 0.3989422804014327
    )


def dot(a, b, dims=((1,), (0,))):
    return lax.dot_general(a, b, (dims, ((), ())), preferred_element_type=F32)


ROOT_HALF = 0.7071067811865476


def gelu(v):
    return 0.5 * v * (1.0 + lax.erf(v * ROOT_HALF))


def send(src, dst, send_sem, recv_sem, device):
    copy = pltpu.make_async_remote_copy(
        src_ref=src,
        dst_ref=dst,
        send_sem=send_sem,
        recv_sem=recv_sem,
        device_id=device,
        device_id_type=MESH,
    )
    copy.start()
    return copy


def halo_copies(pad, rows, count, sems):
    me = lax.axis_index("bins")
    step = DILATION_STEP
    up = pltpu.make_async_remote_copy(
        src_ref=pad.at[pl.ds(rows, step)],
        dst_ref=pad.at[pl.ds(0, step)],
        send_sem=sems.at[0],
        recv_sem=sems.at[1],
        device_id={"bins": lax.rem(me + 1, count)},
        device_id_type=MESH,
    )
    down = pltpu.make_async_remote_copy(
        src_ref=pad.at[pl.ds(step, step)],
        dst_ref=pad.at[pl.ds(rows + step, step)],
        send_sem=sems.at[2],
        recv_sem=sems.at[3],
        device_id={"bins": lax.rem(me + count - 1, count)},
        device_id_type=MESH,
    )
    return up, down


def halo_start(pad, rows, count, sems):
    me = lax.axis_index("bins")
    up, down = halo_copies(pad, rows, count, sems)

    @pl.when(me < count - 1)
    def _():
        up.start()

    @pl.when(me > 0)
    def _():
        down.start()

    @pl.when(me == 0)
    def _():
        pad[0:DILATION_STEP] = jnp.zeros((DILATION_STEP, pad.shape[1]), pad.dtype)

    @pl.when(me == count - 1)
    def _():
        pad[rows + DILATION_STEP : rows + 2 * DILATION_STEP] = jnp.zeros(
            (DILATION_STEP, pad.shape[1]), pad.dtype
        )


def halo_wait(pad, rows, count, sems):
    me = lax.axis_index("bins")
    up, down = halo_copies(pad, rows, count, sems)

    @pl.when(me < count - 1)
    def _():
        up.wait_send()
        down.wait_recv()

    @pl.when(me > 0)
    def _():
        down.wait_send()
        up.wait_recv()


def meet(groups):
    barrier = pltpu.get_barrier_semaphore()
    total = 0
    for axis, devices in groups:
        total += len(devices)
        for device in devices:
            pl.semaphore_signal(barrier, inc=1, device_id={axis: device}, device_id_type=MESH)
    pl.semaphore_wait(barrier, total)


def front_kernel(
    count, pairs, f_ref, gain_ref, taps_ref, ow_ref, hits_ref, goal_ref,
    conv_ref, active_ref, out_ref, all_ref, arrived_ref,
    pad, picked, held, own, halo_sem, local, send_a, recv_a, send_b, recv_b, send_c, recv_c,
):
    rows, channels = f_ref.shape
    hid = ow_ref.shape[0]
    own_rows = own.shape[0]
    step = DILATION_STEP
    me = lax.axis_index("bins")
    spot, at = place("batch", 2)
    others = [lax.rem(me + s, count) for s in range(1, count)]
    peers = [lax.rem(spot + s, pairs) for s in range(1, pairs)]
    meet([("bins", others), ("batch", [at(p) for p in peers])])

    goals = [
        send(goal_ref.at[p], arrived_ref.at[spot], send_a.at[i], recv_a.at[i], {"batch": at(p)})
        for i, p in enumerate(peers)
    ]
    mine = pltpu.make_async_copy(goal_ref.at[spot], arrived_ref.at[spot], local)
    mine.start()

    def norm(i):
        here = pl.ds(pl.multiple_of(i * step, step), step)
        wide = f_ref[here, :].astype(F32)
        inverse = lax.rsqrt(jnp.mean(wide * wide, axis=-1, keepdims=True) + 1e-06)
        pad[pl.ds(pl.multiple_of(i * step + step, step), step), :] = gelu(
            wide * inverse * gain_ref[...]
        ).astype(BF)

    norm(0)
    norm(rows // step - 1)
    halo_start(pad, rows, count, halo_sem)
    pl.loop(1, rows // step - 1)(norm)
    halo_wait(pad, rows, count, halo_sem)

    @pl.loop(0, hid // 256)
    def _(i):
        here = pl.ds(pl.multiple_of(i * 256, 256), 256)
        total = jnp.zeros((rows, 256), F32)
        for tap in range(3):
            total = total + dot(pad[tap * step : tap * step + rows, :], taps_ref[tap, :, here])
        conv_ref[:, here] = total
        active_ref[:, here] = gelu(total).astype(BF)

    @pl.loop(0, channels // 256)
    def _(i):
        here = pl.ds(pl.multiple_of(i * 256, 256), 256)
        block = f_ref[:, here].astype(F32) + dot(active_ref[...], ow_ref[:, here])
        block = block.astype(BF)
        out_ref[:, here] = block
        rows_of = dot(hits_ref[...], block).astype(BF)
        for j in range(count):
            picked[j, :, here] = rows_of[j * own_rows : (j + 1) * own_rows]

    legs = [
        send(picked.at[p], held.at[i], send_b.at[i], recv_b.at[i], {"bins": p})
        for i, p in enumerate(others)
    ]
    total = picked[me].astype(F32)
    for i, leg in enumerate(legs):
        leg.wait_recv()
        total = total + held[i].astype(F32)
    own[...] = total.astype(BF)
    spread = [
        send(own, all_ref.at[spot], send_c.at[i], recv_c.at[i], {"batch": at(p)})
        for i, p in enumerate(peers)
    ]
    all_ref[spot] = own[...]
    mine.wait()
    for leg in legs:
        leg.wait_send()
    for copy in goals + spread:
        copy.wait()


def front(features, gain, taps, out_weight, hits, goals):
    count = lax.axis_size("bins")
    pairs = goals.shape[0]
    rows, channels = features.shape
    hid = out_weight.shape[0]
    own_rows = hits.shape[0] // count
    dma = pltpu.SemaphoreType.DMA
    return pl.pallas_call(
        functools.partial(front_kernel, count, pairs),
        out_shape=(
            jax.ShapeDtypeStruct((rows, hid), F32),
            jax.ShapeDtypeStruct((rows, hid), BF),
            jax.ShapeDtypeStruct((rows, channels), BF),
            jax.ShapeDtypeStruct((pairs, own_rows, channels), BF),
            jax.ShapeDtypeStruct(goals.shape, F32),
        ),
        in_specs=[vmem()] * 6,
        out_specs=(vmem(),) * 5,
        scratch_shapes=[
            pltpu.VMEM((rows + 2 * DILATION_STEP, channels), BF),
            pltpu.VMEM((count, own_rows, channels), BF),
            pltpu.VMEM((count, own_rows, channels), BF),
            pltpu.VMEM((own_rows, channels), BF),
            dma((4,)),
            dma,
            dma((pairs,)),
            dma((pairs,)),
            dma((count,)),
            dma((count,)),
            dma((pairs,)),
            dma((pairs,)),
        ],
        compiler_params=pltpu.CompilerParams(
            collective_id=1, has_side_effects=True, vmem_limit_bytes=20 * 1024 * 1024
        ),
    )(features, gain.reshape(1, channels), taps, out_weight, hits, goals)


def tail_kernel(
    count, batch, f_ref, gain_ref, taps_ref, ow_ref, conv_ref, a_ref, g_ref, parts_ref,
    ig_ref, og_ref,
    pad, hidden_grad, out1, in1, out2, in2, bsum, held, osum,
    halo_sem, send1, recv1, send2, recv2, send3, recv3, send4, recv4,
):
    rows, channels = f_ref.shape
    hid = ow_ref.shape[0]
    high = osum.shape[0]
    step_rows = DILATION_STEP
    me = lax.axis_index("bins")
    seq = lax.axis_index("batch")
    others = [lax.rem(me + s, count) for s in range(1, count)]
    peers = [lax.rem(seq + s, batch) for s in range(1, batch)]
    meet([("bins", others), ("batch", peers)])
    half = count // 2
    spot, parity = lax.div(me, 2), lax.rem(me, 2)
    buddy = 2 * spot + 1 - parity
    quarters = [lax.rem(spot + step, half) for step in range(half)]
    order = list(range(1, half)) + [0]

    def term(part):
        return dot(a_ref[...], parts_ref[part], ((0,), (0,)))

    first = {}
    for step in order:
        out1[step] = term(2 * quarters[step] + 1 - parity).astype(BF)
        first[step] = send(
            out1.at[step], in1.at[step], send1.at[step], recv1.at[step], {"bins": buddy}
        )

    @pl.loop(0, hid // 256)
    def _(i):
        here = pl.ds(pl.multiple_of(i * 256, 256), 256)
        grad = dot(g_ref[...], ow_ref[here, :], ((1,), (1,))) * gelu_slope(conv_ref[:, here])
        pad[step_rows : step_rows + rows, here] = grad.astype(BF)

    halo_start(pad, rows, count, halo_sem)

    second = {}
    for step in order:
        total = term(2 * quarters[step] + parity)
        first[step].wait_recv()
        total = total + in1[step].astype(F32)
        if step:
            out2[step] = total.astype(BF)
            second[step] = send(
                out2.at[step],
                in2.at[step],
                send2.at[step],
                recv2.at[step],
                {"bins": 2 * quarters[step] + parity},
            )
        else:
            out2[0] = total.astype(BF)

    halo_wait(pad, rows, count, halo_sem)

    @pl.loop(0, channels // 256)
    def _(i):
        here = pl.ds(pl.multiple_of(i * 256, 256), 256)
        total = jnp.zeros((rows, 256), F32)
        for tap in range(3):
            shift = (2 - tap) * step_rows
            total = total + dot(
                pad[shift : shift + rows, :], taps_ref[tap, here, :], ((1,), (1,))
            )
        hidden_grad[:, here] = total

    @pl.loop(0, rows // step_rows)
    def _(i):
        here = pl.ds(pl.multiple_of(i * step_rows, step_rows), step_rows)
        wide = f_ref[here, :].astype(F32)
        inverse = lax.rsqrt(jnp.mean(wide * wide, axis=-1, keepdims=True) + 1e-06)
        gain = gain_ref[...]
        normed_grad = hidden_grad[here, :] * gelu_slope(wide * inverse * gain) * gain
        back = inverse * normed_grad - wide * (inverse * inverse * inverse) * jnp.mean(
            normed_grad * wide, axis=-1, keepdims=True
        )
        ig_ref[here, :] = (g_ref[here, :].astype(F32) + back).astype(BF)

    for step in range(1, half):
        second[step].wait_recv()
    for j in range(batch):
        part = out2[0, j * high : (j + 1) * high].astype(F32)
        for step in range(1, half):
            part = part + in2[step, j * high : (j + 1) * high].astype(F32)
        bsum[j] = part.astype(BF)
    third = [
        send(bsum.at[p], held.at[i], send3.at[i], recv3.at[i], {"batch": p})
        for i, p in enumerate(peers)
    ]
    total = bsum[seq].astype(F32)
    for i, copy in enumerate(third):
        copy.wait_recv()
        total = total + held[i].astype(F32)
    osum[...] = total.astype(BF)
    fourth = [
        send(osum, og_ref.at[me], send4.at[i], recv4.at[i], {"bins": p})
        for i, p in enumerate(others)
    ]
    og_ref[me] = osum[...]
    for step in range(half):
        first[step].wait_send()
    for step in range(1, half):
        second[step].wait_send()
    for copy in third:
        copy.wait_send()
    for copy in fourth:
        copy.wait()


def tail(features, gain, taps, out_weight, conv_sum, active, grad, parts):
    count, rows, wide = parts.shape
    batch = lax.axis_size("batch")
    channels = features.shape[1]
    hid = active.shape[1]
    half = count // 2
    high = hid // batch
    dma = pltpu.SemaphoreType.DMA
    return pl.pallas_call(
        functools.partial(tail_kernel, count, batch),
        out_shape=(
            jax.ShapeDtypeStruct((rows, channels), BF),
            jax.ShapeDtypeStruct((count, high, wide), BF),
        ),
        in_specs=[vmem()] * 8,
        out_specs=(vmem(),) * 2,
        scratch_shapes=[
            pltpu.VMEM((rows + 2 * DILATION_STEP, hid), BF),
            pltpu.VMEM((rows, channels), F32),
        ]
        + [pltpu.VMEM((half, hid, wide), BF) for _ in range(4)]
        + [
            pltpu.VMEM((batch, high, wide), BF),
            pltpu.VMEM((batch, high, wide), BF),
            pltpu.VMEM((high, wide), BF),
            dma((4,)),
        ]
        + [dma((half,)) for _ in range(4)]
        + [dma((batch,)) for _ in range(2)]
        + [dma((count,)) for _ in range(2)],
        compiler_params=pltpu.CompilerParams(
            collective_id=6, has_side_effects=True, vmem_limit_bytes=28 * 1024 * 1024
        ),
    )(features, gain.reshape(1, channels), taps, out_weight, conv_sum, active, grad, parts)


def middle_kernel(
    count, pairs, out_ref, all_ref, head_ref, other_ref, goal_ref, sums_ref, hits_ref,
    perm_row_ref, perm_col_ref,
    bg_ref, parts_ref,
    partner, maps, rowgrad, pieces, held, own, seq, mirrored,
    send_m, recv_m, send_a, recv_a, send_b, recv_b,
):
    rows, channels = out_ref.shape
    part = head_ref.shape[1]
    own_rows = own.shape[0]
    wide = parts_ref.shape[2]
    me = lax.axis_index("bins")
    spot, at = place("batch", 2)
    others = [lax.rem(me + s, count) for s in range(1, count)]
    peers = [lax.rem(spot + s, pairs) for s in range(1, pairs)]
    meet([("bins", others), ("batch", [at(p) for p in peers])])

    mirror = send(out_ref, partner, send_m, recv_m, {"bins": count - 1 - me})

    picked = all_ref[...].reshape(pairs * own_rows, channels)
    for side, weight in enumerate((head_ref, other_ref)):
        logits = dot(picked, weight[...])
        predicted = jnp.maximum(logits, 0.0) + jnp.log1p(jnp.exp(-jnp.abs(logits)))
        covered = dot(sums_ref[...], predicted.astype(BF))
        goal = goal_ref[:, side * part : (side + 1) * part]
        spread = (1.0 - goal / (1.0 + covered)).astype(BF)
        back = dot(sums_ref[...], spread, ((0,), (0,)))
        rowgrad[side] = (back * jax.nn.sigmoid(logits)).astype(BF)

    @pl.loop(0, channels // 256)
    def _(i):
        here = pl.ds(pl.multiple_of(i * 256, 256), 256)
        grad = dot(rowgrad[0], head_ref[here, :], ((1,), (1,)))
        grad = (grad + dot(rowgrad[1], other_ref[here, :], ((1,), (1,)))).astype(BF)
        for j in range(pairs):
            pieces[j, :, here] = grad[j * own_rows : (j + 1) * own_rows]

    legs = [
        send(pieces.at[p], held.at[i], send_a.at[i], recv_a.at[i], {"batch": at(p)})
        for i, p in enumerate(peers)
    ]

    @pl.loop(0, channels // 256)
    def _(i):
        here = pl.ds(pl.multiple_of(i * 256, 256), 256)
        down = lax.broadcasted_iota(jnp.int32, (channels, 256), 0)
        along = lax.broadcasted_iota(jnp.int32, (channels, 256), 1) + i * 256
        first = jnp.where(down == perm_row_ref[:, here], 1.0, 0.0)
        second = jnp.where(along == perm_col_ref[...], 1.0, 0.0)
        maps[:, here] = (first + second).astype(BF)

    total = pieces[spot].astype(F32)
    for i, leg in enumerate(legs):
        leg.wait_recv()
        total = total + held[i].astype(F32)
    own[...] = total.astype(BF)
    spread_out = [
        send(own, seq.at[me], send_b.at[i], recv_b.at[i], {"bins": p})
        for i, p in enumerate(others)
    ]
    seq[me] = own[...]

    mirror.wait()
    flip = jnp.where(
        lax.broadcasted_iota(jnp.int32, (rows, rows), 0)
        + lax.broadcasted_iota(jnp.int32, (rows, rows), 1)
        == rows - 1,
        1.0,
        0.0,
    ).astype(BF)
    mirrored[...] = dot(flip, partner[...]).astype(BF)
    for copy in spread_out:
        copy.wait()

    @pl.loop(0, channels // 256)
    def _(i):
        here = pl.ds(pl.multiple_of(i * 256, 256), 256)
        grads = seq[:, :, here].reshape(count * own_rows, 256)
        block = dot(hits_ref[...], grads, ((0,), (0,))) + out_ref[:, here].astype(F32)
        bg_ref[:, here] = (block - 0.5 * dot(mirrored[...], maps[:, here])).astype(BF)

    for j in range(count):
        parts_ref[j] = bg_ref[:, j * wide : (j + 1) * wide]
    for leg in legs:
        leg.wait_send()


def middle(block_out, all_picked, head, other, goals, sums, hits, perm):
    count = lax.axis_size("bins")
    pairs, own_rows, channels = all_picked.shape
    rows = block_out.shape[0]
    part = head.shape[1]
    dma = pltpu.SemaphoreType.DMA
    return pl.pallas_call(
        functools.partial(middle_kernel, count, pairs),
        out_shape=(
            jax.ShapeDtypeStruct((rows, channels), BF),
            jax.ShapeDtypeStruct((count, rows, channels // count), BF),
        ),
        in_specs=[vmem()] * 9,
        out_specs=(vmem(),) * 2,
        scratch_shapes=[
            pltpu.VMEM((rows, channels), BF),
            pltpu.VMEM((channels, channels), BF),
            pltpu.VMEM((2, pairs * own_rows, part), BF),
            pltpu.VMEM((pairs, own_rows, channels), BF),
            pltpu.VMEM((pairs, own_rows, channels), BF),
            pltpu.VMEM((own_rows, channels), BF),
            pltpu.VMEM((count, own_rows, channels), BF),
            pltpu.VMEM((rows, channels), BF),
            dma,
            dma,
            dma((pairs,)),
            dma((pairs,)),
            dma((count,)),
            dma((count,)),
        ],
        compiler_params=pltpu.CompilerParams(
            collective_id=3, has_side_effects=True, vmem_limit_bytes=20 * 1024 * 1024
        ),
    )(
        block_out, all_picked, head, other, goals, sums, hits,
        perm.reshape(1, channels), perm.reshape(channels, 1),
    )


def per_device(
    features,
    norm_gain,
    taps,
    out_weight,
    head_weight,
    rc_perm,
    exon_bins,
    exon_count,
    gene_strand,
    gene_target,
):
    bin_devices = lax.axis_size("bins")
    batch_devices = lax.axis_size("batch")
    bin_index = lax.axis_index("bins")
    rows, channels = features.shape[1:]
    hid = taps.shape[2]
    genes, exons = exon_bins.shape[1:]
    own_genes = gene_target.shape[1]
    tracks = gene_target.shape[2]
    part = head_weight.shape[1]
    own_rows = own_genes * exons

    other_head = lax.ppermute(
        head_weight, "batch", [(i, i ^ 1) for i in range(batch_devices)]
    )
    own_strand = lax.dynamic_slice_in_dim(gene_strand[0], bin_index * own_genes, own_genes, 0)
    own_count = lax.dynamic_slice_in_dim(exon_count[0], bin_index * own_genes, own_genes, 0)
    target = gene_target[0]
    lane = lax.broadcasted_iota(jnp.int32, target.shape, 1)
    swapped = jnp.where(lane % 2 == 0, jnp.roll(target, -1, axis=1), jnp.roll(target, 1, axis=1))
    target = jnp.where(own_strand[:, None] == 1, swapped, target)
    pairs = batch_devices // 2
    odd = lax.rem(lax.axis_index("batch"), 2)
    pieces = target.reshape(own_genes, pairs, 2, part)
    pieces = jnp.where(odd == 1, pieces[:, :, ::-1], pieces)
    pieces = pieces.reshape(own_genes, pairs, 2 * part).transpose(1, 0, 2)
    counted = jnp.broadcast_to(own_count.astype(F32)[None, :, None], (pairs, own_genes, 128))
    positions = bin_index * rows + jnp.arange(rows, dtype=jnp.int32)
    listed = jnp.arange(exons, dtype=jnp.int32)[None, :] < exon_count[0][:, None]
    hits = (
        (exon_bins[0][:, :, None] == positions[None, None, :]) & listed[:, :, None]
    ).reshape(genes * exons, rows).astype(BF)
    conv_sum, active, block_out, all_picked, arrived = front(
        features[0], norm_gain, taps, out_weight, hits, jnp.concatenate([pieces, counted], axis=2)
    )
    gene_rows = pairs * own_genes
    goals = arrived[:, :, : 2 * part].reshape(gene_rows, 2 * part)
    row_count = arrived[:, :, 2 * part].reshape(gene_rows, 1).astype(jnp.int32)
    row = lax.broadcasted_iota(jnp.int32, (gene_rows, gene_rows * exons), 1)
    gene = lax.broadcasted_iota(jnp.int32, (gene_rows, gene_rows * exons), 0)
    sums = ((row // exons == gene) & (row % exons < row_count)).astype(BF)
    block_grad, grad_parts = middle(
        block_out, all_picked, head_weight, other_head, goals, sums, hits, rc_perm
    )
    input_grad, own_parts = tail(
        features[0],
        norm_gain,
        taps,
        out_weight,
        conv_sum,
        active,
        block_grad,
        grad_parts,
    )
    out_weight_grad = own_parts.transpose(1, 0, 2).reshape(hid // batch_devices, channels)
    out_weight_grad = out_weight_grad.astype(F32)
    return (input_grad[None], out_weight_grad)


def solution(mesh):
    in_specs = (
        P("batch", "bins", None),
        P(),
        P(),
        P(),
        P(None, "batch"),
        P(),
        P("batch", None, None),
        P("batch", None),
        P("batch", None),
        P("batch", "bins", None),
    )
    out_specs = (P("batch", "bins", None), P("batch", None))
    return jax.shard_map(
        per_device, mesh=mesh, in_specs=in_specs, out_specs=out_specs, check_vma=False
    )
```
